128 devices in a mesh: seq: 4 (over x), ctx: 16 (over y_hi, z, core), exp: 2 (over y_lo).
Axes of the slice: x: 4, y: 4 (y_hi: 2, y_lo: 2; y = y_hi * 2 + y_lo), z: 4, core: 2. Of those that a mesh axis runs over, the one named last changes fastest.
Arguments:
- tokens: bfloat16 [8, 2048, 768], P(('seq', 'exp'), 'ctx'), may hold values from -6 to 6
- cotangent: bfloat16 [8, 2048, 768], P(('seq', 'exp'), 'ctx'), may hold values from -6 to 6
- routes: int32 [8, 2048, 2], P(('seq', 'exp'), 'ctx'), may hold values from 0 to 63, all different within a row; in each aligned block of 128 rows (0 to 127, 128 to 255, ..., all dimensions but the last counted through in order) at most 8 rows name the same one
- w_query: bfloat16 [768, 768], P(('seq', 'ctx', 'exp')), may hold values from -0.21875 to 0.21875
- w_key: bfloat16 [768, 768], P(('seq', 'ctx', 'exp')), may hold values from -0.21875 to 0.21875
- w_value: bfloat16 [768, 768], P(('seq', 'ctx', 'exp')), may hold values from -0.21875 to 0.21875
- w_output: bfloat16 [768, 768], P(('seq', 'ctx', 'exp')), may hold values from -4 to 4
- w_router: bfloat16 [768, 64], P(('seq', 'ctx', 'exp')), may hold values from -0.15625 to 0.15625
- gain_attn: bfloat16 [768], P(('seq', 'ctx', 'exp')), may hold values from 0.5 to 1.5
- gain_ffn: bfloat16 [768], P(('seq', 'ctx', 'exp')), may hold values from 0.5 to 1.5
- bias_table: float32 [32, 12], replicated, may hold values from -3 to 3
- w_in: bfloat16 [64, 768, 3072], P(('seq', 'ctx'), None, 'exp'), may hold values from -0.21875 to 0.21875
- w_out: bfloat16 [64, 3072, 768], P(('seq', 'ctx'), 'exp'), may hold values from -0.21875 to 0.21875
Outputs:
- out: bfloat16 [8, 2048, 768], P(('seq', 'exp'), 'ctx')
- grad_tokens: float32 [8, 2048, 768], P(('seq', 'exp'), 'ctx')
- grad_query: float32 [768, 768], P(('seq', 'ctx', 'exp'))
- grad_key: float32 [768, 768], P(('seq', 'ctx', 'exp'))
- grad_value: float32 [768, 768], P(('seq', 'ctx', 'exp'))
- grad_output: float32 [768, 768], P(('seq', 'ctx', 'exp'))
- grad_router: float32 [768, 64], P(('seq', 'ctx', 'exp'))
- grad_gain_attn: float32 [768], P(('seq', 'ctx', 'exp'))
- grad_gain_ffn: float32 [768], P(('seq', 'ctx', 'exp'))
- grad_table: float32 [32, 12], replicated
- grad_in: float32 [64, 768, 3072], P(('seq', 'ctx'), None, 'exp')
- grad_out: float32 [64, 3072, 768], P(('seq', 'ctx'), 'exp')
The draws below stay inside these ranges and needn't reach their ends.
Inputs may be any that keep to these rules, and one draw needn't show every extreme that they name: `routes`: each row names 2 different experts. Within each aligned block of 128 rows of a sequence (the rows of one device) no expert is named more than 8 times, a bound that some block reaches.
All inputs are finite; a program needn't handle non-finite values.
Results may differ from the reference program's by a relative error of at most 0.02.
Values may be sent and summed in bfloat16 or wider, within the bound.
No kernel may reach another device: no remote copies, remote signals or barrier semaphores. Data moves between devices by JAX's collectives and lax.ppermute only.
A program may use at most 192 MiB of HBM per device.

```python
import math
import jax
import jax.numpy as jnp
import numpy as np
from jax import lax

D = 768
HEADS = 12
HEAD = 64
FF = 3072
TOP = 2
BUCKETS = 32
MAXDIST = 128
SEQ_LEN = 2048
TOK_DEV = 128
BLK = 64
SEQS = 8
EXPERTS = 64
CAP = 8
N_CTX = 16


def shard_levels(own_key, extent, split, least, high):
    level = 1.0
    for dim, parts in split:
        steps = jax.random.uniform(jax.random.fold_in(jax.random.fold_in(own_key, 6), dim), (parts,), jnp.float32, least / len(split), high / len(split))
        level = level * jnp.repeat(jnp.exp(steps), extent[dim] // parts).reshape((-1,) + (1,) * (len(extent) - 1 - dim))
    return level


def assign_block(own_key, own, number, rows, number_of, top, reach, slope):
    order = jax.random.permutation(own_key, number_of)
    packed, common = portions_of(number_of, rows * top, reach, slope, True), portions_of(number_of, rows * top, reach, slope, False)
    places = jnp.arange(number_of)

    def named(lengths, offset_by):
        used = int((lengths > 0).sum())
        fixed = max(1, used // 4)
        moved = fixed + (places - fixed + offset_by * (used - fixed)) % max(1, number_of - fixed)
        return jnp.zeros((number_of,), jnp.int32).at[order[jnp.where(places < fixed, places, moved)]].set(jnp.asarray(lengths, jnp.int32))

    lengths = jnp.where(number % 4 == 0, named(packed, number // 4), named(common, number - number // 4 - 1))
    mixed = jax.random.permutation(jax.random.fold_in(own, 3), number_of)
    giver, sink = mixed[0:number_of // 2 * 2:2], mixed[1:number_of // 2 * 2:2]
    margin = jnp.minimum(lengths[giver] - 1, reach - lengths[sink]) // 2
    margin = jnp.where((giver == order[0]) | (sink == order[0]) | (lengths[sink] == 0), 0, jnp.maximum(margin, 0))
    moved = jax.random.randint(jax.random.fold_in(own, 4), (number_of // 2,), 0, 1 << 20) % (margin + 1)
    lengths = lengths.at[giver].add(-moved).at[sink].add(moved)
    members = jnp.searchsorted(jnp.cumsum(lengths), jnp.arange(rows * top), side="right").astype(jnp.int32)
    table = members.reshape(top, rows).T
    table = table[jax.random.permutation(jax.random.fold_in(own, 1), rows)]
    offset_by = jax.random.randint(jax.random.fold_in(own, 2), (rows, 1), 0, top)
    return jnp.take_along_axis(table, (jnp.arange(top)[None, :] + offset_by) % top, axis=1)


def portions_of(amount, total, bound, skew, full):
    weights = [(1 << 20) // math.isqrt(rank ** skew) + 1 for rank in range(1, amount + 1)]
    largest = bound if full else min(bound, max(-(-total // amount), total * weights[0] // sum(weights)))
    least = 1 if total - largest >= amount - 1 else 0
    counts, spare = [largest] + [least] * (amount - 1), total - largest - least * (amount - 1)
    while spare > 0:
        movable = [i for i in range(1, amount) if counts[i] < largest] or [i for i in range(1, amount) if counts[i] < bound]
        pool, left = sum([weights[i] for i in movable]), spare
        for i in movable:
            more = min(bound - counts[i], max(1, left * weights[i] // pool), spare)
            counts[i] = counts[i] + more
            spare = spare - more
    return np.array(counts)


def scatter_about(key, dims, width, bound, cuts=(), kind=jnp.bfloat16):
    loudness = shard_levels(key, dims, cuts, -0.22, 0.18) if cuts else 1.0
    values = jax.random.normal(key, dims, jnp.float32) * width * loudness
    return jnp.minimum(jnp.maximum(values, -bound), bound).astype(kind)


def setup_inputs(seed: int = 0) -> dict:
    seeds = jax.random.split(jax.random.key(seed), 14)
    tokens = scatter_about(seeds[0], (SEQS, SEQ_LEN, D), 1.0, 6.0, ((0, 8), (1, 16)))
    cotangent = scatter_about(seeds[1], (SEQS, SEQ_LEN, D), 1.0, 6.0, ((0, 8), (1, 16)))
    routes_keys = jax.random.split(jax.random.fold_in(seeds[2], 1), SEQS * SEQ_LEN // TOK_DEV)
    routes_turns = jax.random.permutation(jax.random.fold_in(seeds[2], 3), SEQS * SEQ_LEN // TOK_DEV)
    routes = jax.vmap(lambda own, number: assign_block(jax.random.fold_in(seeds[2], 2), own, number, TOK_DEV, EXPERTS, TOP, CAP, 1))(routes_keys, routes_turns).reshape((SEQS, SEQ_LEN, TOP))
    w_query = scatter_about(seeds[3], (D, D), D ** -0.5, 0.21875, ((0, 128),))
    w_key = scatter_about(seeds[4], (D, D), D ** -0.5, 0.21875, ((0, 128),))
    w_value = scatter_about(seeds[5], (D, D), D ** -0.5, 0.21875, ((0, 128),))
    w_output = scatter_about(seeds[6], (D, D), (max(1, 7 * D // SEQ_LEN)) ** -0.5, 4.0, ((0, 128),))
    w_router = scatter_about(seeds[7], (D, EXPERTS), (2 * D) ** -0.5, 0.15625, ((0, 128),))
    gain_attn = jnp.clip(1.0 + 0.1 * jax.random.normal(seeds[8], (D,), jnp.float32), 0.5, 1.5).astype(jnp.bfloat16)
    gain_ffn = jnp.clip(1.0 + 0.1 * jax.random.normal(seeds[9], (D,), jnp.float32), 0.5, 1.5).astype(jnp.bfloat16)
    bias_table = scatter_about(seeds[10], (BUCKETS, HEADS), 0.5, 3.0, (), jnp.float32)
    w_in = scatter_about(seeds[11], (EXPERTS, D, FF), D ** -0.5, 0.21875, ((0, 64), (2, 2)))
    w_out = scatter_about(seeds[12], (EXPERTS, FF, D), (FF // 4) ** -0.5, 0.21875, ((0, 64), (1, 2)))
    return {"tokens": tokens, "cotangent": cotangent, "routes": routes, "w_query": w_query, "w_key": w_key, "w_value": w_value, "w_output": w_output, "w_router": w_router, "gain_attn": gain_attn, "gain_ffn": gain_ffn, "bias_table": bias_table, "w_in": w_in, "w_out": w_out}


epsilon = 1e-06
precise = lax.Precision.HIGHEST

@jax.custom_vjp
def low(v):
    return lax.optimization_barrier(v.astype(jnp.bfloat16)).astype(jnp.float32)

@jax.custom_vjp
def low_back(v):
    return v

def low_keep(v):
    return (low(v), None)

def low_pass(kept, grad):
    return (grad,)

def back_keep(v):
    return (v, None)

def back_low(kept, grad):
    return (low(grad),)
low.defvjp(low_keep, low_pass)
low_back.defvjp(back_keep, back_low)

def limits():
    exact_cut = BUCKETS // 2
    borders = []
    for bucket_step in range(1, BUCKETS):
        if bucket_step <= exact_cut:
            borders.append(bucket_step)
        else:
            borders.append(int(math.ceil(exact_cut * (MAXDIST / exact_cut) ** ((bucket_step - exact_cut) / exact_cut))))
    return borders

def bucket_of(distance):
    counted = jnp.zeros(distance.shape, jnp.int32)
    for border in limits():
        counted = counted + (distance >= border).astype(jnp.int32)
    return counted

def stored_positions(length, per_device, half_block, ctx_count):
    row_ids = jnp.arange(length, dtype=jnp.int32)
    slab_ids = row_ids // per_device
    within = row_ids % per_device
    block_ids = jnp.where(within < half_block, slab_ids, 2 * ctx_count - 1 - slab_ids)
    return block_ids * half_block + within % half_block

def matmul(first_op, second_op):
    return jnp.dot(first_op, second_op, precision=precise, preferred_element_type=jnp.float32)

def attention(queries, key_rows, values, bias_table, places):
    rows_block = min(512, SEQ_LEN)
    keys_heads = key_rows.reshape(SEQ_LEN, HEADS, HEAD)
    values_heads = values.reshape(SEQ_LEN, HEADS, HEAD)

    def one_block(pieces):
        query_rows, query_places = pieces
        distance = query_places[:, None] - places[None, :]
        biases = jnp.moveaxis(bias_table[bucket_of(distance)], -1, 0)
        scores = jnp.einsum('qhd,khd->hqk', query_rows.reshape(rows_block, HEADS, HEAD), keys_heads, precision=precise) * HEAD ** (-0.5) + biases
        scores = low_back(scores)
        scores = jnp.where(distance[None] >= 0, scores, -1000000000.0)
        weights = low(jax.nn.softmax(scores, axis=-1))
        merged = jnp.einsum('hqk,khd->qhd', weights, values_heads, precision=precise)
        return merged.reshape(rows_block, HEADS * HEAD)
    blocks = lax.map(jax.checkpoint(one_block), (queries.reshape(-1, rows_block, HEADS * HEAD), places.reshape(-1, rows_block)))
    return blocks.reshape(SEQ_LEN, HEADS * HEAD)

def expert_rows(routes):
    per_block = routes.reshape(N_CTX, TOK_DEV * TOP)
    route_marks = (per_block[:, :, None] == jnp.arange(EXPERTS, dtype=jnp.int32)).astype(jnp.int32)
    earlier = jnp.cumsum(route_marks, axis=1, dtype=jnp.int32) - route_marks
    slot_ids = lax.optimization_barrier(jnp.sum(earlier * route_marks, axis=-1, dtype=jnp.int32))
    block_ids = jnp.arange(N_CTX, dtype=jnp.int32)[:, None]
    return (per_block * (N_CTX * CAP) + block_ids * CAP + slot_ids).reshape(SEQ_LEN, TOP)

def sequence_forward(source, routes, w_query, w_key, w_value, w_output, w_router, gain_attn, gain_ffn, bias_table, w_in, w_out):
    places = stored_positions(SEQ_LEN, TOK_DEV, BLK, N_CTX)
    inv_first = lax.rsqrt(lax.optimization_barrier(jnp.mean(source * source, axis=-1, keepdims=True)) + epsilon)
    normed = low(source * inv_first * gain_attn)
    queries = low(low_back(matmul(normed, w_query)))
    key_rows = low(low_back(matmul(normed, w_key)))
    values = low(low_back(matmul(normed, w_value)))
    attended = low(low_back(attention(queries, key_rows, values, bias_table, places)))
    hidden = source + low_back(matmul(attended, w_output))
    inv_second = lax.rsqrt(lax.optimization_barrier(jnp.mean(hidden * hidden, axis=-1, keepdims=True)) + epsilon)
    normed_ffn = low(hidden * inv_second * gain_ffn)
    logits = matmul(normed_ffn, w_router)
    route_marks = (routes[:, :, None] == jnp.arange(EXPERTS, dtype=jnp.int32)).astype(jnp.float32)
    chosen = lax.optimization_barrier(jnp.sum(route_marks * logits[:, None, :], axis=-1))
    gate_weights = jax.nn.softmax(chosen, axis=-1)
    targets = expert_rows(routes).reshape(-1)
    copies = jnp.broadcast_to(normed_ffn[:, None, :], (SEQ_LEN, TOP, D)).reshape(-1, D)
    buffers = jnp.zeros((EXPERTS * N_CTX * CAP, D), jnp.float32).at[targets].set(copies).reshape(EXPERTS, N_CTX * CAP, D)
    pre_act = low_back(jnp.einsum('erd,edf->erf', buffers, w_in, precision=precise))
    inner_act = low(jax.nn.gelu(pre_act, approximate=True))
    results = low(low_back(jnp.einsum('erf,efd->erd', inner_act, w_out, precision=precise)))
    picked = results.reshape(-1, D)[targets].reshape(SEQ_LEN, TOP, D)
    return hidden + lax.optimization_barrier(jnp.sum(gate_weights[:, :, None] * picked, axis=1))

def reference(tokens, cotangent, routes, w_query, w_key, w_value, w_output, w_router, gain_attn, gain_ffn, bias_table, w_in, w_out):
    weight_list = tuple((member.astype(jnp.float32) for member in (w_query, w_key, w_value, w_output, w_router, gain_attn, gain_ffn, bias_table, w_in, w_out)))

    def one_sequence(totals, pieces):
        seq_tokens, seq_routes, seq_cotangent = pieces
        result, pullback = jax.vjp(lambda inputs, weights: sequence_forward(inputs, seq_routes, *weights), seq_tokens.astype(jnp.float32), weight_list)
        grad_inputs, grad_weights = pullback(seq_cotangent.astype(jnp.float32))
        totals = jax.tree.map(lambda first_op, second_op: first_op + second_op, totals, grad_weights)
        return (totals, (result.astype(jnp.bfloat16), grad_inputs))
    empty_grads = jax.tree.map(jnp.zeros_like, weight_list)
    totals, (outputs, grad_tokens) = lax.scan(one_sequence, empty_grads, (tokens, routes, cotangent))
    return (outputs, grad_tokens, totals[0], totals[1], totals[2], totals[3], totals[4], totals[5], totals[6], totals[7], totals[8], totals[9])
```

```python
import functools
import math

import jax
import jax.numpy as jnp
import numpy as np
from jax import lax
from jax.experimental import pallas as pl
from jax.experimental.pallas import tpu as pltpu
from jax.sharding import Mesh
from jax.sharding import PartitionSpec as P

HEADS = 12
HEAD = 64
TOP = 2
BUCKETS = 32
MAXDIST = 128
WIDTH = HEADS * HEAD
HALF = WIDTH // 2
PAIRS = HALF // 128
SIDE_GAIN = 64
SIDE_END = WIDTH + 128
FAR_LANE = 2 * 128 - 127
TILE = 128
CHUNK = 256
CORE = "ctx_2"
CHIPS = ("ctx_0", "ctx_1")
SAME_CORE = ("exp", "seq", "ctx_0", "ctx_1")
QUAD = ("ctx_2", "exp")
SEQ_CTX_EXP = ("seq", "ctx_0", "ctx_1", "ctx_2", "exp")
CTX = ("ctx_0", "ctx_1", "ctx_2")
SEQ_CTX = ("seq", "ctx_0", "ctx_1", "ctx_2")
BLOCKED = -1000000000.0
epsilon = 1e-06
precise = lax.Precision.HIGHEST


def limits():
    exact_cut = BUCKETS // 2
    borders = []
    for bucket_step in range(1, BUCKETS):
        if bucket_step <= exact_cut:
            borders.append(bucket_step)
        else:
            borders.append(
                int(
                    math.ceil(
                        exact_cut * (MAXDIST / exact_cut) ** ((bucket_step - exact_cut) / exact_cut)
                    )
                )
            )
    return borders


def rows_dot(first_op, second_op):
    return lax.dot_general(
        first_op, second_op, (((0,), (0,)), ((), ())), preferred_element_type=jnp.float32
    )


def cols_dot(first_op, second_op):
    return lax.dot_general(
        first_op, second_op, (((1,), (1,)), ((), ())), preferred_element_type=jnp.float32
    )


def plain_dot(first_op, second_op):
    return jnp.dot(first_op, second_op, preferred_element_type=jnp.float32)


def own_tiles(place_ref):
    first = place_ref[0]
    return first, 15 - first


def fill_bias(bias_full, place_ref):
    tile_a, tile_b = own_tiles(place_ref)

    def fill(tile, carry):
        at = pl.ds(pl.multiple_of(tile * TILE, TILE), TILE)
        bias_full[0:256, at] = jnp.full((256, TILE), jnp.where(tile <= tile_a, 0.0, BLOCKED))
        bias_full[256:512, at] = jnp.full((256, TILE), jnp.where(tile <= tile_b, 0.0, BLOCKED))
        return carry

    lax.fori_loop(0, 16, fill, 0)


def near_kernel(table_ref, near_ref):
    row = lax.broadcasted_iota(jnp.int32, (TILE, 2 * TILE), 0)
    column = lax.broadcasted_iota(jnp.int32, (TILE, 2 * TILE), 1)
    distance = row + TILE - column
    for head in range(2 * PAIRS):
        last = table_ref[BUCKETS - 1, head]
        bias = jnp.full(distance.shape, table_ref[0, head] - last)
        for bucket, border in enumerate(limits()):
            bias = jnp.where(distance >= border, table_ref[bucket + 1, head] - last, bias)
        rows = slice(TILE * (head % 2), TILE * (head % 2) + TILE)
        near_ref[head // 2, rows, :] = jnp.where(distance >= 0, bias, BLOCKED)


def near_bias(bias_full, near_ref, place_ref, pair):
    tile_a, tile_b = own_tiles(place_ref)
    for rows, tile in ((slice(0, 256), tile_a), (slice(256, 512), tile_b)):
        bias_full[rows, pl.ds(pl.multiple_of(tile * TILE, TILE), TILE)] = near_ref[pair, :, TILE:]

        @pl.when(tile > 0)
        def _():
            before = pl.ds(pl.multiple_of((tile - 1) * TILE, TILE), TILE)
            bias_full[rows, before] = near_ref[pair, :, :TILE]


def by_head(rows):
    left = lax.broadcasted_iota(jnp.int32, (TILE, TILE), 1) < HEAD
    rows = rows.astype(jnp.float32)
    parts = []
    for tile in (rows[:TILE], rows[TILE:]):
        parts.append(jnp.where(left, tile, 0.0))
        parts.append(jnp.where(left, 0.0, tile))
    return jnp.concatenate(parts, axis=0)


def side_by_side(four):
    left = lax.broadcasted_iota(jnp.int32, (TILE, TILE), 1) < HEAD
    return (
        jnp.where(left, four[:TILE], four[TILE : 2 * TILE]),
        jnp.where(left, four[2 * TILE : 3 * TILE], four[3 * TILE :]),
    )


def chunk_rows(chunk):
    return slice(0, 512) if chunk < 4 else slice(256, 512)


def pair_lanes(pair):
    return pl.ds(pl.multiple_of(pair * 128, 128), 128)


def side_row(weights_ref, lane):
    return jnp.concatenate(
        [
            jnp.transpose(
                weights_ref[0, 128 * step : 128 * step + 128, WIDTH:].astype(jnp.float32)
            )[lane : lane + 1]
            for step in range(WIDTH // 128)
        ],
        axis=1,
    )


def attend_kernel(
    place_ref,
    mine_ref,
    other_ref,
    weights_ref,
    near_ref,
    normed_ref,
    q_ref,
    k_ref,
    v_ref,
    att_ref,
    lse_ref,
    bias_full,
    scores,
):
    tile_a, tile_b = own_tiles(place_ref)
    core = place_ref[1]
    gain = side_row(weights_ref, SIDE_GAIN)
    for from_ref, from_core in ((mine_ref, core), (other_ref, 1 - core)):

        def norm_one(chip, carry):
            for half in range(2):
                source = from_ref[chip, 64 * half : 64 * half + 64, :].astype(jnp.float32)
                inv = lax.rsqrt(jnp.mean(source * source, axis=-1, keepdims=True) + epsilon)
                block = 2 * chip + from_core if half == 0 else 31 - 2 * chip - from_core
                normed_ref[pl.ds(pl.multiple_of(block * 64, 64), 64), :] = (
                    source * inv * gain
                ).astype(jnp.bfloat16)
            return carry

        lax.fori_loop(0, 8, norm_one, 0)

    def project(chunk, carry):
        at = pl.ds(pl.multiple_of(chunk * 512, 512), 512)
        rows = normed_ref[at, :]
        k_ref[at, :] = plain_dot(rows, weights_ref[0, :, HALF:WIDTH]).astype(jnp.bfloat16)
        v_ref[at, :] = plain_dot(rows, weights_ref[1, :, :HALF]).astype(jnp.bfloat16)
        return carry

    lax.fori_loop(0, 4, project, 0)
    own = jnp.concatenate(
        [
            normed_ref[pl.ds(pl.multiple_of(tile_a * TILE, TILE), TILE), :],
            normed_ref[pl.ds(pl.multiple_of(tile_b * TILE, TILE), TILE), :],
        ],
        axis=0,
    )
    q_ref[...] = plain_dot(own, weights_ref[0, :, :HALF]).astype(jnp.bfloat16)
    fill_bias(bias_full, place_ref)

    def one_pair(pair, carry):
        near_bias(bias_full, near_ref, place_ref, pair)
        lanes = pair_lanes(pair)
        query = (by_head(q_ref[:, lanes]) * HEAD**-0.5).astype(jnp.bfloat16)
        top = None
        for chunk in range(8):
            rows, at = chunk_rows(chunk), slice(chunk * CHUNK, (chunk + 1) * CHUNK)
            part = cols_dot(query[rows], k_ref[at, lanes]) + bias_full[rows, at]
            scores[rows, at] = part
            here = jnp.maximum(part[:, :128], part[:, 128:])
            if chunk == 0:
                top = here
            elif chunk < 4:
                top = jnp.maximum(top, here)
            else:
                top = jnp.concatenate([top[:256], jnp.maximum(top[256:], here)], axis=0)
        top = jnp.max(top, axis=-1, keepdims=True)
        total, merged = None, None
        for chunk in range(8):
            rows, at = chunk_rows(chunk), slice(chunk * CHUNK, (chunk + 1) * CHUNK)
            raised = jnp.exp(scores[rows, at] - top[rows])
            here = raised[:, :128] + raised[:, 128:]
            product = plain_dot(raised.astype(jnp.bfloat16), v_ref[at, lanes])
            if chunk == 0:
                total, merged = here, product
            elif chunk < 4:
                total, merged = total + here, merged + product
            else:
                total = jnp.concatenate([total[:256], total[256:] + here], axis=0)
                merged = jnp.concatenate([merged[:256], merged[256:] + product], axis=0)
        total = jnp.sum(total, axis=-1, keepdims=True)
        lse_ref[pair] = top + jnp.log(total)
        first, second = side_by_side(merged / total)
        first, second = first.astype(jnp.bfloat16), second.astype(jnp.bfloat16)
        att_ref[0, 0:64, lanes] = first[:64]
        att_ref[1, 0:64, lanes] = first[64:]
        att_ref[1, 64:128, lanes] = second[:64]
        att_ref[0, 64:128, lanes] = second[64:]
        return carry

    lax.fori_loop(0, PAIRS, one_pair, 0)


def core_rows(core):
    return pl.ds(pl.multiple_of(core * HALF, 128), HALF)


def mid_kernel(
    place_ref,
    mine_ref,
    other_ref,
    tokens_ref,
    weights_ref,
    wo_other_ref,
    pack_ref,
    hidden_ref,
    normed_ref,
    packed_ref,
):
    core = place_ref[1]
    mine, other = mine_ref[core], other_ref[core]
    mine_rows, other_rows = core_rows(core), core_rows(1 - core)
    hidden_ref[:, mine_rows] = plain_dot(
        mine, weights_ref[1, mine_rows, HALF:WIDTH]
    ) + plain_dot(other, weights_ref[1, other_rows, HALF:WIDTH])
    hidden_ref[:, other_rows] = plain_dot(mine, wo_other_ref[mine_rows, :]) + plain_dot(
        other, wo_other_ref[other_rows, :]
    )
    hidden = tokens_ref[...].astype(jnp.float32) + hidden_ref[...]
    hidden_ref[...] = hidden
    inv = lax.rsqrt(jnp.mean(hidden * hidden, axis=-1, keepdims=True) + epsilon)
    normed = (hidden * inv * side_row(weights_ref, SIDE_GAIN + 1)).astype(jnp.bfloat16)
    normed_ref[...] = normed
    packed_ref[...] = plain_dot(pack_ref[...], normed).astype(jnp.bfloat16)


def token_kernel(
    back_ref,
    pick_ref,
    hidden_ref,
    normed_ref,
    cot_ref,
    routes_ref,
    weights_ref,
    out_ref,
    d_hidden_ref,
    d_mixed_ref,
    sums_ref,
):
    picked = plain_dot(pick_ref[...], back_ref[...])
    side = weights_ref[0, :, WIDTH:]
    logits = plain_dot(normed_ref[...], side)
    lane = lax.broadcasted_iota(jnp.int32, (TILE, 128), 1)
    routes = routes_ref[...]
    marks = [lane == routes[:, k : k + 1] for k in range(TOP)]
    chosen = [jnp.sum(jnp.where(mark, logits, 0.0), axis=-1, keepdims=True) for mark in marks]
    top = jnp.maximum(*chosen)
    raised = [jnp.exp(one - top) for one in chosen]
    gates = [one / (raised[0] + raised[1]) for one in raised]
    rows = [
        picked[TILE * k : TILE * k + TILE, :WIDTH].astype(jnp.bfloat16).astype(jnp.float32)
        for k in range(TOP)
    ]
    hidden = hidden_ref[...]
    out_ref[...] = (hidden + (gates[0] * rows[0] + gates[1] * rows[1])).astype(jnp.bfloat16)
    grad_top = cot_ref[...].astype(jnp.float32)
    d_gates = [jnp.sum(grad_top * one, axis=-1, keepdims=True) for one in rows]
    mean_gate = gates[0] * d_gates[0] + gates[1] * d_gates[1]
    d_logits = sum(
        jnp.where(mark, gate * (d_gate - mean_gate), 0.0)
        for mark, gate, d_gate in zip(marks, gates, d_gates)
    ).astype(jnp.bfloat16)
    d_normed = picked[:TILE, WIDTH:] + picked[TILE:, WIDTH:] + cols_dot(d_logits, side)
    inv = lax.rsqrt(jnp.mean(hidden * hidden, axis=-1, keepdims=True) + epsilon)
    scaled = side_row(weights_ref, SIDE_GAIN + 1) * d_normed
    d_hidden = (
        grad_top
        + inv * scaled
        - hidden * (inv * inv * inv) * jnp.mean(scaled * hidden, axis=-1, keepdims=True)
    )
    d_hidden_ref[...] = d_hidden
    d_mixed_ref[...] = d_hidden.astype(jnp.bfloat16)
    d_gain = jnp.sum(d_normed * hidden * inv, axis=0, keepdims=True)
    d_router = rows_dot(normed_ref[...], d_logits)
    for step in range(WIDTH // 128):
        at = slice(128 * step, 128 * step + 128)
        column = jnp.transpose(jnp.broadcast_to(d_gain[:, at], (128, 128)))
        sums_ref[at, :] = jnp.where(lane == SIDE_GAIN, column, d_router[at]).astype(jnp.bfloat16)


def tile_order(ref, lanes):
    return jnp.concatenate(
        [ref[0, 0:64, lanes], ref[1, 0:64, lanes], ref[1, 64:128, lanes], ref[0, 64:128, lanes]],
        axis=0,
    )


def by_distance(tiles):
    row = lax.broadcasted_iota(jnp.int32, tiles.shape, 0)
    for bit in range(7):
        moved = pltpu.roll(tiles, 2 * TILE - (1 << bit), 1)
        tiles = jnp.where((row & (1 << bit)) != 0, moved, tiles)
    return jnp.sum(tiles, axis=0, keepdims=True)


def back_kernel(
    place_ref,
    q_ref,
    k_ref,
    v_ref,
    att_ref,
    mixed_ref,
    mixed_other_ref,
    lse_ref,
    near_ref,
    normed_t_ref,
    att_t_ref,
    side_ref,
    weights_ref,
    wo_other_ref,
    dq_ref,
    dk_ref,
    dv_ref,
    sums_ref,
    bias_full,
    d_scores,
    profile,
    d_mixed,
    d_att,
):
    tile_a, tile_b = own_tiles(place_ref)
    core = place_ref[1]
    fill_bias(bias_full, place_ref)
    d_mixed[core] = mixed_ref[...]
    d_mixed[1 - core] = mixed_other_ref[...]
    d_att[...] = (
        cols_dot(
            tile_order(d_mixed, core_rows(core)), weights_ref[1, core_rows(core), HALF:WIDTH]
        )
        + cols_dot(tile_order(d_mixed, core_rows(1 - core)), wo_other_ref[core_rows(core), :])
    ).astype(jnp.bfloat16)

    def one_pair(pair, carry):
        near_bias(bias_full, near_ref, place_ref, pair)
        lanes = pair_lanes(pair)
        query = (by_head(q_ref[:, lanes]) * HEAD**-0.5).astype(jnp.bfloat16)
        grads = by_head(d_att[:, lanes])
        outs = by_head(tile_order(att_ref, lanes))
        row_dots = jnp.sum(grads * outs, axis=-1, keepdims=True)
        grads = grads.astype(jnp.bfloat16)
        lse = lse_ref[pair]
        total, dq = None, None
        for chunk in range(8):
            rows, at = chunk_rows(chunk), slice(chunk * CHUNK, (chunk + 1) * CHUNK)
            keys, values = k_ref[at, lanes], v_ref[at, lanes]
            probs = jnp.exp(cols_dot(query[rows], keys) + bias_full[rows, at] - lse[rows])
            d_part = probs * (cols_dot(grads[rows], values) - row_dots[rows])
            low = d_part.astype(jnp.bfloat16)
            d_scores[rows, at] = d_part
            dv_ref[at, lanes] = rows_dot(probs.astype(jnp.bfloat16), grads[rows]).astype(
                jnp.bfloat16
            )
            dk_ref[at, lanes] = rows_dot(low, query[rows]).astype(jnp.bfloat16)
            product = plain_dot(low, keys)
            here = d_part[:, :128] + d_part[:, 128:]
            if chunk == 0:
                total, dq = here, product
            elif chunk < 4:
                total, dq = total + here, dq + product
            else:
                total = jnp.concatenate([total[:256], total[256:] + here], axis=0)
                dq = jnp.concatenate([dq[:256], dq[256:] + product], axis=0)
        first, second = side_by_side(dq * HEAD**-0.5)
        dq_ref[0:128, lanes] = first.astype(jnp.bfloat16)
        dq_ref[128:256, lanes] = second.astype(jnp.bfloat16)
        total = total[:256] + total[256:]
        at_b = pl.ds(pl.multiple_of(tile_b * TILE, TILE), TILE)
        before_b = pl.ds(pl.multiple_of((tile_b - 1) * TILE, TILE), TILE)
        at_a = pl.ds(pl.multiple_of(tile_a * TILE, TILE), TILE)
        before_a = pl.ds(pl.multiple_of(jnp.maximum(tile_a - 1, 0) * TILE, TILE), TILE)
        own = d_scores[0:256, at_a] + d_scores[256:512, at_b]
        before = d_scores[256:512, before_b] + jnp.where(
            tile_a > 0, d_scores[0:256, before_a], 0.0
        )
        far = total - own - before
        for head in range(2):
            rows = slice(TILE * head, TILE * head + TILE)
            sums = by_distance(jnp.concatenate([before[rows], own[rows]], axis=1))
            rest = jnp.sum(far[rows], keepdims=True)
            lane = lax.broadcasted_iota(jnp.int32, (1, 2 * TILE), 1)
            sums = sums + jnp.where(lane == FAR_LANE, rest, 0.0)
            high = sums.astype(jnp.bfloat16).astype(jnp.float32)
            for step, part in enumerate((high, sums - high)):
                for half in range(2):
                    cell = part[:, TILE * half : TILE * half + TILE]
                    row = 4 * (2 * pair + head) + 2 * step + half
                    profile[pl.ds(row, 1), :] = cell
                    profile[pl.ds(row + 24, 1), :] = cell
        return carry

    lax.fori_loop(0, PAIRS, one_pair, 0)

    own_t = jnp.concatenate(
        [
            normed_t_ref[:, pl.ds(pl.multiple_of(tile_a * TILE, TILE), TILE)],
            normed_t_ref[:, pl.ds(pl.multiple_of(tile_b * TILE, TILE), TILE)],
        ],
        axis=1,
    )
    sums_ref[0, :, :HALF] = plain_dot(own_t, dq_ref[...]).astype(jnp.bfloat16)
    sums_ref[0, :, WIDTH:] = side_ref[...]
    pair_mixed = jnp.concatenate([d_mixed[0, :, core_rows(core)], d_mixed[1, :, core_rows(core)]])
    sums_ref[1, :, HALF:WIDTH] = plain_dot(att_t_ref[...], pair_mixed).astype(jnp.bfloat16)
    sums_ref[0, :, HALF:WIDTH] = plain_dot(normed_t_ref[...], dk_ref[...]).astype(jnp.bfloat16)
    sums_ref[1, :, :HALF] = plain_dot(normed_t_ref[...], dv_ref[...]).astype(jnp.bfloat16)
    cells = profile[...].astype(jnp.bfloat16)
    for step in range(WIDTH // 48):
        sums_ref[1, 48 * step : 48 * step + 48, WIDTH:] = cells


def spread_kernel(place_ref, dq_ref, dk_ref, dv_ref, weights_ref, kept_ref, given_ref):
    tile_a, _ = own_tiles(place_ref)
    core = place_ref[1]

    low = jnp.bfloat16

    def keep(slab_core, chip, row, lanes, part):
        @pl.when(core == slab_core)
        def _():
            kept_ref[chip, row : row + 64, lanes] = part

        @pl.when(core != slab_core)
        def _():
            given_ref[chip, row : row + 64, lanes] = part

    for column in range(WIDTH // CHUNK):
        lanes = slice(column * CHUNK, (column + 1) * CHUNK)
        part = cols_dot(dk_ref[...], weights_ref[0, lanes, HALF:WIDTH]) + cols_dot(
            dv_ref[...], weights_ref[1, lanes, :HALF]
        )
        part = part.astype(low)
        for block in range(32):
            slab = block if block < 16 else 31 - block
            row = 0 if block < 16 else 64
            keep(slab % 2, slab // 2, row, lanes, part[64 * block : 64 * block + 64])
    dqn = cols_dot(dq_ref[...], weights_ref[0, :, :HALF])
    for step, (slab_core, row) in enumerate(((0, 0), (1, 0), (1, 64), (0, 64))):
        for ref, wanted in ((kept_ref, core == slab_core), (given_ref, core != slab_core)):

            @pl.when(wanted)
            def _():
                ref[tile_a, row : row + 64, :] = (
                    ref[tile_a, row : row + 64, :].astype(jnp.float32)
                    + dqn[64 * step : 64 * step + 64]
                ).astype(low)


def up_kernel(place_ref, cot_ref, w_out_ref, up_ref):
    def one_block(block, carry):
        at = pl.ds(pl.multiple_of(block * 512, 512), 512)
        up_ref[at, :] = cols_dot(cot_ref[at, :WIDTH], w_out_ref[...]).astype(jnp.bfloat16)
        return carry

    lax.fori_loop(0, cot_ref.shape[0] // 512, one_block, 0)


def expert_kernel(
    place_ref,
    rows_ref,
    cot_ref,
    up_ref,
    w_in_ref,
    w_out_ref,
    weights_ref,
    back_ref,
    inner_ref,
    d_pre_ref,
    d_expert_ref,
):
    expert = place_ref[2]
    block_rows = 512
    lane = lax.broadcasted_iota(jnp.int32, (block_rows, 128), 1)

    def one_block(block, carry):
        at = pl.ds(pl.multiple_of(block * block_rows, block_rows), block_rows)
        rows = rows_ref[at, :]
        logits = plain_dot(rows, weights_ref[0, :, WIDTH:])
        partner = cot_ref[at, WIDTH:].astype(jnp.float32)
        own = jnp.sum(jnp.where(lane == expert, logits, 0.0), axis=-1, keepdims=True)
        also = jnp.sum(
            jnp.where(lane.astype(jnp.float32) == partner, logits, 0.0), axis=-1, keepdims=True
        )
        top = jnp.maximum(own, also)
        own, also = jnp.exp(own - top), jnp.exp(also - top)
        gate = own / (own + also)
        d_expert_ref[at, :] = (gate * cot_ref[at, :WIDTH].astype(jnp.float32)).astype(jnp.bfloat16)
        for step in range(6):
            lanes = slice(256 * step, 256 * step + 256)
            value, slope = gelu_parts(plain_dot(rows, w_in_ref[:, lanes]))
            inner_ref[at, lanes] = value.astype(jnp.bfloat16)
            d_pre_ref[at, lanes] = (
                gate * up_ref[at, lanes].astype(jnp.float32) * slope
            ).astype(jnp.bfloat16)
        back_ref[at, :WIDTH] = plain_dot(inner_ref[at, :], w_out_ref[...]).astype(jnp.bfloat16)
        back_ref[at, WIDTH:] = cols_dot(d_pre_ref[at, :], w_in_ref[...]).astype(jnp.bfloat16)
        return carry

    lax.fori_loop(0, rows_ref.shape[0] // block_rows, one_block, 0)


def call(kernel, shapes, scratch, flops, place, *operands):
    outs = tuple(jax.ShapeDtypeStruct(shape, dtype) for shape, dtype in shapes)
    specs = [pl.BlockSpec(memory_space=pltpu.VMEM) for _ in operands]
    if place is not None:
        specs, operands = [pl.BlockSpec(memory_space=pltpu.SMEM)] + specs, (place, *operands)
    return pl.pallas_call(
        kernel,
        out_shape=outs,
        in_specs=specs,
        out_specs=tuple(pl.BlockSpec(memory_space=pltpu.VMEM) for _ in outs),
        scratch_shapes=[pltpu.VMEM(shape, dtype) for shape, dtype in scratch],
        compiler_params=pltpu.CompilerParams(vmem_limit_bytes=60 * 2**20),
        cost_estimate=pl.CostEstimate(
            flops=flops, bytes_accessed=16 * 2**20, transcendentals=3 * 10**6
        ),
    )(*operands)


ROWS = 16 * TILE


def near_biases(table):
    shapes = (((PAIRS, 2 * TILE, 2 * TILE), jnp.float32),)
    return call(near_kernel, shapes, (), 10**7, table)[0]


def attend(*operands):
    low, full = jnp.bfloat16, jnp.float32
    shapes = (
        ((ROWS, WIDTH), low),
        ((2 * TILE, HALF), low),
        ((ROWS, HALF), low),
        ((ROWS, HALF), low),
        ((2, TILE, HALF), low),
        ((PAIRS, 4 * TILE, 1), full),
    )
    scratch = (((4 * TILE, ROWS), full), ((4 * TILE, ROWS), full))
    return call(attend_kernel, shapes, scratch, 8 * 10**9, *operands)


def attend_back(*operands):
    low, full = jnp.bfloat16, jnp.float32
    shapes = (
        ((2 * TILE, HALF), low),
        ((ROWS, HALF), low),
        ((ROWS, HALF), low),
        ((2, WIDTH, SIDE_END), low),
    )
    scratch = (
        ((4 * TILE, ROWS), full),
        ((4 * TILE, ROWS), full),
        ((48, TILE), full),
        ((2, TILE, WIDTH), low),
        ((2 * TILE, HALF), low),
    )
    return call(back_kernel, shapes, scratch, 12 * 10**9, *operands)


def mid(rows, *operands):
    low, full = jnp.bfloat16, jnp.float32
    shapes = (((TILE, WIDTH), full), ((TILE, WIDTH), low), ((rows, WIDTH), low))
    return call(mid_kernel, shapes, (), 10**9, *operands)


def token_side(*operands):
    low, full = jnp.bfloat16, jnp.float32
    shapes = (
        ((TILE, WIDTH), low),
        ((TILE, WIDTH), full),
        ((TILE, WIDTH), low),
        ((WIDTH, 128), low),
    )
    return call(token_kernel, shapes, (), 10**9, None, *operands)


def up_pass(rows, hidden_units, *operands):
    (up,) = call(up_kernel, (((rows, hidden_units), jnp.bfloat16),), (), 3 * 10**9, *operands)
    return up


def spread(*operands):
    shapes = (((8, TILE, WIDTH), jnp.bfloat16),) * 2
    return call(spread_kernel, shapes, (), 3 * 10**9, *operands)


def expert_pass(rows, hidden_units, *operands):
    low = jnp.bfloat16
    shapes = (
        ((rows, 2 * WIDTH), low),
        ((rows, hidden_units), low),
        ((rows, hidden_units), low),
        ((rows, WIDTH), low),
    )
    return call(expert_kernel, shapes, (), 8 * 10**9, *operands)


def swap(shard):
    return lax.ppermute(shard, CORE, [(0, 1), (1, 0)])


def to_all(shard, axes):
    devices = lax.axis_size(axes)
    return lax.all_to_all(
        jnp.broadcast_to(shard[None], (devices, *shard.shape)), axes, 0, 0, tiled=True
    )


def quad_exchange(blocks):
    me = lax.axis_index(QUAD)
    got = [lax.dynamic_index_in_dim(blocks, me, 0, keepdims=False)]
    for step in range(1, 4):
        part = lax.dynamic_index_in_dim(blocks, me ^ step, 0, keepdims=False)
        got.append(lax.ppermute(part, QUAD, [(i, i ^ step) for i in range(4)]))
    rows = []
    for place in range(4):
        row = got[0]
        for step in range(1, 4):
            row = jnp.where(me ^ step == place, got[step], row)
        rows.append(row)
    return jnp.stack(rows)


def exchange(blocks, axes):
    return lax.all_to_all(blocks, axes, split_axis=0, concat_axis=0, tiled=True)


def gelu_parts(pre):
    root = math.sqrt(2.0 / math.pi)
    square = pre * pre
    curve = jnp.tanh(pre * (root + (root * 0.044715) * square))
    share = 0.5 + 0.5 * curve
    value = pre * share
    slope = share + value * (1.0 - share) * (2 * root + (6 * root * 0.044715) * square)
    return value, slope


def shards(
    tokens,
    cotangent,
    routes,
    w_query,
    w_key,
    w_value,
    w_output,
    w_router,
    gain_attn,
    gain_ffn,
    bias_table,
    w_in,
    w_out,
):
    f32, bf16 = jnp.float32, jnp.bfloat16
    core = lax.axis_index(CORE)
    chip = lax.axis_index(CHIPS)
    expert = lax.axis_index(SEQ_CTX)
    on_first = core == 0
    tok_count, model_width = tokens.shape[1:]
    local_rows = w_query.shape[0]
    expert_count = w_router.shape[1]
    place = jnp.stack([chip, core, expert]).astype(jnp.int32)

    own_tokens = tokens[0]
    mine = to_all(own_tokens, CHIPS)
    other = swap(mine)

    quarters = jnp.stack([jnp.stack([w_query, w_key]), jnp.stack([w_value, w_output])])
    quarters = quarters.reshape(2, 2, local_rows, 2, HALF).transpose(3, 0, 2, 1, 4)
    quarters = quarters.reshape(2, 2, local_rows, 2 * HALF)
    extra = jnp.concatenate(
        [
            w_router,
            gain_attn[:, None],
            gain_ffn[:, None],
            jnp.zeros((local_rows, 128 - expert_count - 2), bf16),
        ],
        axis=1,
    )
    extra = jnp.stack([extra, jnp.zeros_like(extra)])
    extra = jnp.broadcast_to(extra[None], (2, *extra.shape))
    packed_weights = jnp.concatenate([quarters, extra], axis=-1).reshape(4, local_rows, -1)
    group_rows = 4 * local_rows
    weight_rows = quad_exchange(packed_weights).reshape(group_rows, -1)
    all_weights = to_all(weight_rows, SAME_CORE).reshape(2, model_width, -1)
    wo_half = all_weights[1, :, HALF:model_width]
    wo_other = swap(wo_half)
    gain_first = all_weights[0, :, model_width + expert_count].astype(f32)[None, :]

    own_table = lax.dynamic_slice_in_dim(bias_table, core * (HEADS // 2), HEADS // 2, 1)
    near = near_biases(own_table)

    route_ids = routes[0]
    capacity = max(2, 2 * TOP * tok_count // expert_count)
    flat_ids = route_ids.reshape(-1)
    flat_marks = (flat_ids[:, None] == jnp.arange(expert_count, dtype=jnp.int32)).astype(jnp.int32)
    earlier = jnp.cumsum(flat_marks, axis=0, dtype=jnp.int32) - flat_marks
    slot_ids = jnp.sum(earlier * flat_marks, axis=-1, dtype=jnp.int32)
    row_index = (flat_ids * capacity + slot_ids).reshape(tok_count, TOP)
    exp_count = lax.axis_size("exp")
    device_count = expert_count * exp_count
    slots = jnp.arange(device_count * capacity, dtype=jnp.int32)
    slots = slots // (exp_count * capacity) * capacity + slots % capacity
    pick = (row_index.T[:, :, None] == slots[None, None, :]).astype(bf16)
    pack = (row_index.T[:, None, :] == slots[None, :, None]).astype(bf16)

    def to_experts(rows):
        return exchange(rows.reshape(device_count, capacity, -1), SEQ_CTX_EXP)

    cot_own = cotangent[0]
    with_partner = [
        jnp.concatenate(
            [cot_own, jnp.broadcast_to(route_ids[:, k : k + 1], (tok_count, 128)).astype(bf16)],
            axis=1,
        )
        for k in (1, 0)
    ]
    cot_there = to_experts(
        plain_dot(
            jnp.concatenate([pack[0], pack[1]], axis=1), jnp.concatenate(with_partner, axis=0)
        ).astype(bf16)
    )

    normed_all, queries, keys, values, attended, log_totals = attend(
        place, mine, other, all_weights, near
    )

    attended_other = swap(attended)
    pair_attended = jnp.concatenate(
        [
            jnp.where(on_first, attended, attended_other),
            jnp.where(on_first, attended_other, attended),
        ],
        axis=-1,
    )
    hidden, normed_ffn, packed = mid(
        device_count * capacity,
        place,
        attended,
        attended_other,
        own_tokens,
        all_weights,
        wo_other,
        pack[0] + pack[1],
    )
    there = to_experts(packed)

    inner_in, inner_out = w_in[0], w_out[0]
    flat_rows = there.reshape(-1, model_width)
    flat_cot = cot_there.reshape(flat_rows.shape[0], -1)
    up = up_pass(flat_rows.shape[0], inner_in.shape[1], place, flat_cot, inner_out)
    sent_back, inner_act, d_pre, d_expert = expert_pass(
        flat_rows.shape[0],
        inner_in.shape[1],
        place,
        flat_rows,
        flat_cot,
        up,
        inner_in,
        inner_out,
        all_weights,
    )
    returned = exchange(sent_back.reshape(device_count, capacity, -1), SEQ_CTX_EXP)
    grad_out_local = rows_dot(inner_act, d_expert)
    grad_in_local = rows_dot(flat_rows, d_pre)

    output, d_hidden, d_mixed, sums_side = token_side(
        returned.reshape(device_count * capacity, -1),
        pick.reshape(TOP * tok_count, -1),
        hidden,
        normed_ffn,
        cot_own,
        route_ids,
        all_weights,
    )
    d_mixed_other = swap(d_mixed)

    d_queries, d_keys, d_values, to_sum = attend_back(
        place,
        queries,
        keys,
        values,
        attended,
        d_mixed,
        d_mixed_other,
        log_totals,
        near,
        normed_all.T,
        pair_attended.reshape(2 * tok_count, model_width).T,
        sums_side,
        all_weights,
        wo_other,
    )
    groups = model_width // group_rows
    summed = exchange(to_sum.reshape(2 * groups, group_rows, -1), SAME_CORE)
    summed = jnp.sum(summed.astype(f32), axis=0)

    kept, given = spread(place, d_queries, d_keys, d_values, all_weights)
    chip_sums = (kept.astype(f32) + swap(given).astype(f32)).astype(bf16)
    d_normed = jnp.sum(exchange(chip_sums, CHIPS).astype(f32), axis=0)
    source = own_tokens.astype(f32)
    inv_first = lax.rsqrt(jnp.mean(source * source, axis=-1, keepdims=True) + epsilon)
    scaled_first = gain_first * d_normed
    grad_tokens = (
        d_hidden
        + inv_first * scaled_first
        - source * inv_first**3 * jnp.mean(scaled_first * source, axis=-1, keepdims=True)
    )

    cells = jnp.broadcast_to(
        summed[None, :, model_width:].reshape(1, 1, -1), (4, 1, 128 * group_rows)
    )
    cells = jnp.pad(cells, ((0, 0), (0, 0), (0, -cells.shape[2] % summed.shape[1])))
    finals = quad_exchange(
        jnp.concatenate(
            [summed.reshape(4, local_rows, -1), cells.reshape(4, -1, summed.shape[1])], axis=1
        )
    )
    finals = finals.reshape(2, 2, -1, summed.shape[1])
    body = finals[:, :, :local_rows]

    def both(part, begin):
        return jnp.concatenate(
            [body[0, part, :, begin : begin + HALF], body[1, part, :, begin : begin + HALF]], axis=1
        )

    grad_query, grad_key, grad_value, grad_output = both(0, 0), both(0, HALF), both(1, 0), both(1, HALF)
    grad_gain_attn = (
        jnp.sum(
            grad_query * w_query.astype(f32)
            + grad_key * w_key.astype(f32)
            + grad_value * w_value.astype(f32),
            axis=1,
        )
        / gain_attn.astype(f32)
    )
    last = body[0, 0, :, model_width:] + body[1, 0, :, model_width:]
    profile = finals[:, 1, local_rows:].reshape(2, -1)[:, : 128 * group_rows]
    profile = profile.reshape(HEADS, 2, 2 * TILE).sum(axis=1)
    far = (TILE - np.arange(2 * TILE)) % (2 * TILE)
    bucket = sum((far >= border).astype(np.int32) for border in limits())
    marks = (bucket[:, None] == np.arange(BUCKETS)).astype(np.float32)
    grad_table = lax.dot_general(
        jnp.asarray(marks), profile, (((0,), (1,)), ((), ())), precision=precise
    )
    return (
        output[None],
        grad_tokens[None],
        grad_query,
        grad_key,
        grad_value,
        grad_output,
        last[:, :expert_count],
        grad_gain_attn,
        last[:, expert_count],
        grad_table,
        grad_in_local[None],
        grad_out_local[None],
    )


def solution(mesh):
    split = Mesh(
        mesh.devices.reshape(mesh.shape["seq"], 2, 4, 2, mesh.shape["exp"]),
        ("seq", "ctx_0", "ctx_1", "ctx_2", "exp"),
    )
    in_specs = (
        P(("seq", "exp"), CTX, None),
        P(("seq", "exp"), CTX, None),
        P(("seq", "exp"), CTX, None),
        P(SEQ_CTX_EXP, None),
        P(SEQ_CTX_EXP, None),
        P(SEQ_CTX_EXP, None),
        P(SEQ_CTX_EXP, None),
        P(SEQ_CTX_EXP, None),
        P(SEQ_CTX_EXP),
        P(SEQ_CTX_EXP),
        P(),
        P(SEQ_CTX, None, "exp"),
        P(SEQ_CTX, "exp", None),
    )
    out_specs = (
        P(("seq", "exp"), CTX, None),
        P(("seq", "exp"), CTX, None),
        P(SEQ_CTX_EXP, None),
        P(SEQ_CTX_EXP, None),
        P(SEQ_CTX_EXP, None),
        P(SEQ_CTX_EXP, None),
        P(SEQ_CTX_EXP, None),
        P(SEQ_CTX_EXP),
        P(SEQ_CTX_EXP),
        P(),
        P(SEQ_CTX, None, "exp"),
        P(SEQ_CTX, "exp", None),
    )
    return jax.shard_map(
        shards, mesh=split, in_specs=in_specs, out_specs=out_specs, check_vma=False
    )
```

```python
import functools
import math

import jax
import jax.numpy as jnp
import numpy as np
from jax import lax
from jax.experimental import pallas as pl
from jax.experimental.pallas import tpu as pltpu
from jax.sharding import Mesh
from jax.sharding import PartitionSpec as P

HEADS = 12
HEAD = 64
TOP = 2
BUCKETS = 32
MAXDIST = 128
WIDTH = HEADS * HEAD
HALF = WIDTH // 2
PAIRS = HALF // 128
SIDE_GAIN = 64
SIDE_END = WIDTH + 128
FAR_LANE = 2 * 128 - 127
EXPERT_BLOCK = 256
EXPERT_VMEM = 60 * 2**20
TILE = 128
CHUNK = 256
CORE = "ctx_2"
CHIPS = ("ctx_0", "ctx_1")
SAME_CORE = ("exp", "seq", "ctx_0", "ctx_1")
QUAD = ("ctx_2", "exp")
SEQ_CTX_EXP = ("seq", "ctx_0", "ctx_1", "ctx_2", "exp")
CTX = ("ctx_0", "ctx_1", "ctx_2")
SEQ_CTX = ("seq", "ctx_0", "ctx_1", "ctx_2")
BLOCKED = -1000000000.0
epsilon = 1e-06
precise = lax.Precision.HIGHEST


def limits():
    exact_cut = BUCKETS // 2
    borders = []
    for bucket_step in range(1, BUCKETS):
        if bucket_step <= exact_cut:
            borders.append(bucket_step)
        else:
            borders.append(
                int(
                    math.ceil(
                        exact_cut * (MAXDIST / exact_cut) ** ((bucket_step - exact_cut) / exact_cut)
                    )
                )
            )
    return borders


def rows_dot(first_op, second_op):
    return lax.dot_general(
        first_op, second_op, (((0,), (0,)), ((), ())), preferred_element_type=jnp.float32
    )


def cols_dot(first_op, second_op):
    return lax.dot_general(
        first_op, second_op, (((1,), (1,)), ((), ())), preferred_element_type=jnp.float32
    )


def plain_dot(first_op, second_op):
    return jnp.dot(first_op, second_op, preferred_element_type=jnp.float32)


def own_tiles(place_ref):
    first = place_ref[0]
    return first, 15 - first


def fill_bias(bias_full, place_ref):
    tile_a, tile_b = own_tiles(place_ref)

    def fill(tile, carry):
        at = pl.ds(pl.multiple_of(tile * TILE, TILE), TILE)
        bias_full[0:256, at] = jnp.full((256, TILE), jnp.where(tile <= tile_a, 0.0, BLOCKED))
        bias_full[256:512, at] = jnp.full((256, TILE), jnp.where(tile <= tile_b, 0.0, BLOCKED))
        return carry

    lax.fori_loop(0, 16, fill, 0)


def near_kernel(table_ref, near_ref):
    row = lax.broadcasted_iota(jnp.int32, (TILE, 2 * TILE), 0)
    column = lax.broadcasted_iota(jnp.int32, (TILE, 2 * TILE), 1)
    distance = row + TILE - column
    for head in range(2 * PAIRS):
        last = table_ref[BUCKETS - 1, head]
        bias = jnp.full(distance.shape, table_ref[0, head] - last)
        for bucket, border in enumerate(limits()):
            bias = jnp.where(distance >= border, table_ref[bucket + 1, head] - last, bias)
        rows = slice(TILE * (head % 2), TILE * (head % 2) + TILE)
        near_ref[head // 2, rows, :] = jnp.where(distance >= 0, bias, BLOCKED)


def near_bias(bias_full, near_ref, place_ref, pair):
    tile_a, tile_b = own_tiles(place_ref)
    for rows, tile in ((slice(0, 256), tile_a), (slice(256, 512), tile_b)):
        bias_full[rows, pl.ds(pl.multiple_of(tile * TILE, TILE), TILE)] = near_ref[pair, :, TILE:]

        @pl.when(tile > 0)
        def _():
            before = pl.ds(pl.multiple_of((tile - 1) * TILE, TILE), TILE)
            bias_full[rows, before] = near_ref[pair, :, :TILE]


def by_head(rows):
    left = lax.broadcasted_iota(jnp.int32, (TILE, TILE), 1) < HEAD
    rows = rows.astype(jnp.float32)
    parts = []
    for tile in (rows[:TILE], rows[TILE:]):
        parts.append(jnp.where(left, tile, 0.0))
        parts.append(jnp.where(left, 0.0, tile))
    return jnp.concatenate(parts, axis=0)


def side_by_side(four):
    left = lax.broadcasted_iota(jnp.int32, (TILE, TILE), 1) < HEAD
    return (
        jnp.where(left, four[:TILE], four[TILE : 2 * TILE]),
        jnp.where(left, four[2 * TILE : 3 * TILE], four[3 * TILE :]),
    )


def later_units(tile_a):
    reach = tile_a // 2
    units = []
    for step in range(1, 4):
        of_first = step <= reach
        chunk = jnp.where(of_first, step, 4 + step - reach)
        units.append((of_first, jnp.where(of_first, 0, 256), chunk))
    return units


def chunk_at(chunk):
    return pl.ds(pl.multiple_of(chunk * CHUNK, CHUNK), CHUNK)


def row_at(first):
    return pl.ds(pl.multiple_of(first, 256), 256)


def pair_lanes(pair):
    return pl.ds(pl.multiple_of(pair * 128, 128), 128)


def side_row(side, lane):
    return jnp.concatenate(
        [
            jnp.transpose(side[128 * step : 128 * step + 128].astype(jnp.float32))[lane : lane + 1]
            for step in range(WIDTH // 128)
        ],
        axis=1,
    )


def attend_kernel(
    place_ref,
    mine_any,
    other_any,
    weights_any,
    near_any,
    normed_any,
    k_any,
    v_any,
    q_ref,
    att_ref,
    lse_ref,
    side_ref,
    bias_full,
    scores,
    query,
    tokens,
    weights_ref,
    near_ref,
    normed_ref,
    k_ref,
    v_ref,
    sems,
):
    load_first = pltpu.make_async_copy(weights_any.at[0], weights_ref.at[0], sems.at[0])
    load_second = pltpu.make_async_copy(weights_any.at[1], weights_ref.at[1], sems.at[1])
    load_near = pltpu.make_async_copy(near_any, near_ref, sems.at[4])
    save_normed = pltpu.make_async_copy(normed_ref, normed_any, sems.at[5])
    save_k = pltpu.make_async_copy(k_ref, k_any, sems.at[6])
    save_v = pltpu.make_async_copy(v_ref, v_any, sems.at[7])
    tile_a, tile_b = own_tiles(place_ref)
    core = place_ref[1]

    def load_tokens(block):
        slab = block if block < 16 else 31 - block
        chip, row = slab // 2, 0 if block < 16 else 64
        copies = []
        for which, (from_any, from_core) in enumerate(((mine_any, core), (other_any, 1 - core))):
            to_block = 2 * chip + from_core if block < 16 else 31 - 2 * chip - from_core
            copies.append(
                pltpu.make_async_copy(
                    from_any.at[chip, row : row + 64],
                    tokens.at[pl.ds(pl.multiple_of(to_block * 64, 64), 64)],
                    sems.at[8 + block // 2 * 2 + which],
                )
            )
        return copies

    load_first.start()
    for block in range(0, 8, 2):
        for copy in load_tokens(block):
            copy.start()
    load_second.start()
    for block in range(8, 32, 2):
        for copy in load_tokens(block):
            copy.start()
    load_near.start()
    fill_bias(bias_full, place_ref)
    load_first.wait()
    side_ref[...] = weights_ref[0, :, WIDTH:]
    gain = side_row(side_ref[...], SIDE_GAIN)

    def norm_part(part):
        for block in range(8 * part, 8 * part + 8, 2):
            for copy in load_tokens(block):
                copy.wait()
            at = slice(64 * block, 64 * block + 128)
            source = tokens[at, :].astype(jnp.float32)
            inv = lax.rsqrt(jnp.mean(source * source, axis=-1, keepdims=True) + epsilon)
            normed_ref[at, :] = (source * inv * gain).astype(jnp.bfloat16)

    norm_part(0)
    load_second.wait()
    for part in range(4):
        if part < 3:
            norm_part(part + 1)
        at = slice(512 * part, 512 * part + 512)
        rows = normed_ref[at, :]
        for to_ref, weight in (
            (k_ref, weights_ref[0, :, HALF:WIDTH]),
            (v_ref, weights_ref[1, :, :HALF]),
        ):
            product = plain_dot(rows, weight).astype(jnp.bfloat16)
            for pair in range(PAIRS):
                to_ref[pair, at, :] = product[:, 128 * pair : 128 * pair + 128]
    save_normed.start()
    save_k.start()
    save_v.start()
    own = jnp.concatenate(
        [
            normed_ref[pl.ds(pl.multiple_of(tile_a * TILE, TILE), TILE), :],
            normed_ref[pl.ds(pl.multiple_of(tile_b * TILE, TILE), TILE), :],
        ],
        axis=0,
    )
    q_ref[...] = plain_dot(own, weights_ref[0, :, :HALF]).astype(jnp.bfloat16)
    load_near.wait()
    units = later_units(tile_a)
    lse_ref[...] = jnp.zeros_like(lse_ref)

    def one_pair(pair, carry):
        near_bias(bias_full, near_ref, place_ref, pair)
        lanes = pair_lanes(pair)
        query[...] = (by_head(q_ref[:, lanes]) * HEAD**-0.5).astype(jnp.bfloat16)

        def widest(part):
            return jnp.maximum(part[:, :128], part[:, 128:])

        both = cols_dot(query[...], k_ref[pair, 0:CHUNK, :]) + bias_full[:, 0:CHUNK]
        scores[0], scores[4] = both[:256], both[256:]
        top_a, top_b = widest(both[:256]), widest(both[256:])
        for chunk in range(1, 5):
            at = slice(chunk * CHUNK, (chunk + 1) * CHUNK)
            part = cols_dot(query[256:512, :], k_ref[pair, at, :]) + bias_full[256:512, at]
            scores[4 + chunk] = part
            top_b = jnp.maximum(top_b, widest(part))
        for step, (of_first, first, chunk) in enumerate(units):
            part = (
                cols_dot(query[row_at(first), :], k_ref[pair, chunk_at(chunk), :])
                + bias_full[row_at(first), chunk_at(chunk)]
            )
            scores[1 + step] = part
            here = widest(part)
            top_a = jnp.maximum(top_a, jnp.where(of_first, here, 2 * BLOCKED))
            top_b = jnp.maximum(top_b, jnp.where(of_first, 2 * BLOCKED, here))
        top_a = jnp.max(top_a, axis=-1, keepdims=True)
        top_b = jnp.max(top_b, axis=-1, keepdims=True)

        def raise_to(part, top, at):
            raised = jnp.exp(part - top)
            return raised[:, :128] + raised[:, 128:], plain_dot(
                raised.astype(jnp.bfloat16), v_ref[pair, at, :]
            )

        total_a, merged_a = raise_to(scores[0], top_a, slice(0, CHUNK))
        total_b, merged_b = raise_to(scores[4], top_b, slice(0, CHUNK))
        for chunk in range(1, 5):
            here, product = raise_to(
                scores[4 + chunk], top_b, slice(chunk * CHUNK, (chunk + 1) * CHUNK)
            )
            total_b, merged_b = total_b + here, merged_b + product
        for step, (of_first, first, chunk) in enumerate(units):
            top = jnp.where(of_first, top_a, top_b)
            here, product = raise_to(scores[1 + step], top, chunk_at(chunk))
            total_a = total_a + jnp.where(of_first, here, 0.0)
            total_b = total_b + jnp.where(of_first, 0.0, here)
            merged_a = merged_a + jnp.where(of_first, product, 0.0)
            merged_b = merged_b + jnp.where(of_first, 0.0, product)
        total_a = jnp.sum(total_a, axis=-1, keepdims=True)
        total_b = jnp.sum(total_b, axis=-1, keepdims=True)
        lane = lax.broadcasted_iota(jnp.int32, (2 * TILE, 128), 1)
        for rows, lse in (
            (slice(0, 256), top_a + jnp.log(total_a)),
            (slice(256, 512), top_b + jnp.log(total_b)),
        ):
            lse_ref[rows, :] = jnp.where(lane == pair, lse, lse_ref[rows, :])
        first, second = side_by_side(
            jnp.concatenate([merged_a / total_a, merged_b / total_b], axis=0)
        )
        first, second = first.astype(jnp.bfloat16), second.astype(jnp.bfloat16)
        att_ref[0, 0:64, lanes] = first[:64]
        att_ref[1, 0:64, lanes] = first[64:]
        att_ref[1, 64:128, lanes] = second[:64]
        att_ref[0, 64:128, lanes] = second[64:]
        return carry

    lax.fori_loop(0, PAIRS, one_pair, 0)
    save_normed.wait()
    save_k.wait()
    save_v.wait()


def core_rows(core):
    return pl.ds(pl.multiple_of(core * HALF, 128), HALF)


def mid_kernel(
    place_ref,
    mine_ref,
    other_ref,
    tokens_ref,
    side_ref,
    wo_mine_ref,
    wo_other_ref,
    pack_ref,
    hidden_ref,
    normed_ref,
    packed_ref,
):
    core = place_ref[1]
    mine, other = mine_ref[core], other_ref[core]
    mine_rows, other_rows = core_rows(core), core_rows(1 - core)
    hidden_ref[:, mine_rows] = plain_dot(
        mine, wo_mine_ref[mine_rows, :]
    ) + plain_dot(other, wo_mine_ref[other_rows, :])
    hidden_ref[:, other_rows] = plain_dot(mine, wo_other_ref[mine_rows, :]) + plain_dot(
        other, wo_other_ref[other_rows, :]
    )
    hidden = tokens_ref[...].astype(jnp.float32) + hidden_ref[...]
    hidden_ref[...] = hidden
    inv = lax.rsqrt(jnp.mean(hidden * hidden, axis=-1, keepdims=True) + epsilon)
    normed = (hidden * inv * side_row(side_ref[...], SIDE_GAIN + 1)).astype(jnp.bfloat16)
    normed_ref[...] = normed
    packed_ref[...] = plain_dot(pack_ref[...], normed).astype(jnp.bfloat16)


def token_kernel(
    back_ref,
    pick_ref,
    hidden_ref,
    normed_ref,
    cot_ref,
    routes_ref,
    side_ref,
    out_ref,
    d_hidden_ref,
    d_mixed_ref,
    sums_ref,
):
    picked = plain_dot(pick_ref[...], back_ref[...])
    side = side_ref[...]
    logits = plain_dot(normed_ref[...], side)
    lane = lax.broadcasted_iota(jnp.int32, (TILE, 128), 1)
    routes = routes_ref[...]
    marks = [lane == routes[:, k : k + 1] for k in range(TOP)]
    chosen = [jnp.sum(jnp.where(mark, logits, 0.0), axis=-1, keepdims=True) for mark in marks]
    top = jnp.maximum(*chosen)
    raised = [jnp.exp(one - top) for one in chosen]
    gates = [one / (raised[0] + raised[1]) for one in raised]
    rows = [
        picked[TILE * k : TILE * k + TILE, :WIDTH].astype(jnp.bfloat16).astype(jnp.float32)
        for k in range(TOP)
    ]
    hidden = hidden_ref[...]
    out_ref[...] = (hidden + (gates[0] * rows[0] + gates[1] * rows[1])).astype(jnp.bfloat16)
    grad_top = cot_ref[...].astype(jnp.float32)
    d_gates = [jnp.sum(grad_top * one, axis=-1, keepdims=True) for one in rows]
    mean_gate = gates[0] * d_gates[0] + gates[1] * d_gates[1]
    d_logits = sum(
        jnp.where(mark, gate * (d_gate - mean_gate), 0.0)
        for mark, gate, d_gate in zip(marks, gates, d_gates)
    ).astype(jnp.bfloat16)
    d_normed = picked[:TILE, WIDTH:] + picked[TILE:, WIDTH:] + cols_dot(d_logits, side)
    inv = lax.rsqrt(jnp.mean(hidden * hidden, axis=-1, keepdims=True) + epsilon)
    scaled = side_row(side, SIDE_GAIN + 1) * d_normed
    d_hidden = (
        grad_top
        + inv * scaled
        - hidden * (inv * inv * inv) * jnp.mean(scaled * hidden, axis=-1, keepdims=True)
    )
    d_hidden_ref[...] = d_hidden
    d_mixed_ref[...] = d_hidden.astype(jnp.bfloat16)
    d_gain = jnp.sum(d_normed * hidden * inv, axis=0, keepdims=True)
    d_router = rows_dot(normed_ref[...], d_logits)
    for step in range(WIDTH // 128):
        at = slice(128 * step, 128 * step + 128)
        column = jnp.transpose(jnp.broadcast_to(d_gain[:, at], (128, 128)))
        sums_ref[at, :] = jnp.where(lane == SIDE_GAIN, column, d_router[at]).astype(jnp.bfloat16)


def tile_order(ref, lanes):
    return jnp.concatenate(
        [ref[0, 0:64, lanes], ref[1, 0:64, lanes], ref[1, 64:128, lanes], ref[0, 64:128, lanes]],
        axis=0,
    )


def by_distance(tiles):
    for half in (64, 32, 16, 8):
        tiles = tiles[:half] + pltpu.roll(tiles[half:], 2 * TILE - half, 1)
    row = lax.broadcasted_iota(jnp.int32, tiles.shape, 0)
    for step in (4, 2, 1):
        moved = pltpu.roll(tiles, 2 * TILE - step, 1)
        tiles = jnp.where((row & step) != 0, moved, tiles)
    return jnp.sum(tiles, axis=0, keepdims=True)


def wide(ref):
    return jnp.concatenate([ref[pair] for pair in range(PAIRS)], axis=1)


def back_kernel(
    place_ref,
    q_ref,
    k_any,
    v_any,
    att_ref,
    mixed_ref,
    mixed_other_ref,
    lse_ref,
    near_any,
    normed_t_any,
    att_t_any,
    side_ref,
    wo_mine_ref,
    wo_other_ref,
    dk_any,
    dv_any,
    sums_any,
    dq_ref,
    bias_full,
    d_scores,
    profile,
    d_mixed,
    d_att,
    query,
    grads,
    row_dots,
    row_lse,
    query_t,
    grads_t,
    dk_t,
    dv_t,
    k_ref,
    v_ref,
    near_ref,
    normed_t_ref,
    att_t_ref,
    dk_ref,
    dv_ref,
    sums_ref,
    sems,
):
    load_normed = pltpu.make_async_copy(normed_t_any, normed_t_ref, sems.at[0])
    load_att = pltpu.make_async_copy(att_t_any, att_t_ref, sems.at[1])
    def saves_of(pair):
        return [
            pltpu.make_async_copy(dk_ref.at[pair], dk_any.at[pair], sems.at[20 + 2 * pair]),
            pltpu.make_async_copy(dv_ref.at[pair], dv_any.at[pair], sems.at[21 + 2 * pair]),
        ]

    def loads_of(pair):
        return [
            pltpu.make_async_copy(from_any.at[pair], to_ref.at[pair], sems.at[8 + 4 * step + pair])
            for step, (from_any, to_ref) in enumerate(
                ((k_any, k_ref), (v_any, v_ref), (near_any, near_ref))
            )
        ]

    saves = [
        pltpu.make_async_copy(sums_ref.at[part], sums_any.at[part], sems.at[4 + part])
        for part in range(2)
    ]
    for pair in range(PAIRS):
        for load in loads_of(pair):
            load.start()
    load_normed.start()
    load_att.start()
    tile_a, tile_b = own_tiles(place_ref)
    core = place_ref[1]
    fill_bias(bias_full, place_ref)
    d_mixed[core] = mixed_ref[...]
    d_mixed[1 - core] = mixed_other_ref[...]
    d_att[...] = (
        cols_dot(tile_order(d_mixed, core_rows(core)), wo_mine_ref[core_rows(core), :])
        + cols_dot(tile_order(d_mixed, core_rows(1 - core)), wo_other_ref[core_rows(core), :])
    ).astype(jnp.bfloat16)
    units = later_units(tile_a)
    reach = tile_a // 2

    def one_pair(pair, carry):
        for load in loads_of(pair):
            load.wait()
        near_bias(bias_full, near_ref, place_ref, pair)
        lanes = pair_lanes(pair)
        query[...] = (by_head(q_ref[:, lanes]) * HEAD**-0.5).astype(jnp.bfloat16)
        some = by_head(d_att[:, lanes])
        outs = by_head(tile_order(att_ref, lanes))
        row_dots[...] = jnp.sum(some * outs, axis=-1, keepdims=True)
        grads[...] = some.astype(jnp.bfloat16)
        lane = lax.broadcasted_iota(jnp.int32, (4 * TILE, 128), 1)
        row_lse[...] = jnp.sum(jnp.where(lane == pair, lse_ref[...], 0.0), axis=-1, keepdims=True)
        rest = slice(5 * CHUNK, 8 * CHUNK)
        dk_t[:, rest] = jnp.zeros((128, 3 * CHUNK), jnp.float32)
        dv_t[:, rest] = jnp.zeros((128, 3 * CHUNK), jnp.float32)
        query_t[...] = jnp.transpose(query[...])
        grads_t[...] = jnp.transpose(grads[...])

        def unit(rows, at):
            keys = k_ref[pair, at, :]
            probs = jnp.exp(
                cols_dot(query[rows, :], keys) + bias_full[rows, at] - row_lse[rows, :]
            )
            d_part = probs * (cols_dot(grads[rows, :], v_ref[pair, at, :]) - row_dots[rows, :])
            low = d_part.astype(jnp.bfloat16)
            d_values = plain_dot(grads_t[:, rows], probs.astype(jnp.bfloat16))
            d_keys = plain_dot(query_t[:, rows], low)
            return d_part, plain_dot(low, keys), d_keys, d_values

        both, dq, d_keys, d_values = unit(slice(0, 512), slice(0, CHUNK))
        d_scores[0], d_scores[4] = both[:256], both[256:]
        dk_t[:, 0:CHUNK] = d_keys
        dv_t[:, 0:CHUNK] = d_values
        dq_a, dq_b = dq[:256], dq[256:]
        total = (both[:256, :128] + both[:256, 128:]) + (both[256:, :128] + both[256:, 128:])
        for chunk in range(1, 5):
            at = slice(chunk * CHUNK, (chunk + 1) * CHUNK)
            part, dq, d_keys, d_values = unit(slice(256, 512), at)
            d_scores[4 + chunk] = part
            dk_t[:, at] = d_keys
            dv_t[:, at] = d_values
            dq_b = dq_b + dq
            total = total + (part[:, :128] + part[:, 128:])
        for step, (of_first, first, chunk) in enumerate(units):
            at = chunk_at(chunk)
            part, dq, d_keys, d_values = unit(row_at(first), at)
            d_scores[1 + step] = part
            dk_t[:, at] = dk_t[:, at] + d_keys
            dv_t[:, at] = dv_t[:, at] + d_values
            dq_a = dq_a + jnp.where(of_first, dq, 0.0)
            dq_b = dq_b + jnp.where(of_first, 0.0, dq)
            total = total + (part[:, :128] + part[:, 128:])
        dk_ref[pair] = jnp.transpose(dk_t[...].astype(jnp.bfloat16))
        dv_ref[pair] = jnp.transpose(dv_t[...].astype(jnp.bfloat16))
        for copy in saves_of(pair):
            copy.start()
        first, second = side_by_side(jnp.concatenate([dq_a, dq_b], axis=0) * HEAD**-0.5)
        dq_ref[0:128, lanes] = first.astype(jnp.bfloat16)
        dq_ref[128:256, lanes] = second.astype(jnp.bfloat16)

        def tile_of(slot, tile):
            return d_scores[slot, :, pl.ds(pl.multiple_of(tile % 2 * TILE, TILE), TILE)]

        def slot_b(tile):
            chunk = tile // 2
            return jnp.where(chunk <= 4, 4 + chunk, chunk - 4 + reach)

        own = tile_of(reach, tile_a) + tile_of(slot_b(tile_b), tile_b)
        ahead = jnp.maximum(tile_a - 1, 0)
        before = tile_of(slot_b(tile_b - 1), tile_b - 1) + jnp.where(
            tile_a > 0, tile_of(ahead // 2, ahead), 0.0
        )
        far = total - own - before
        for head in range(2):
            rows = slice(TILE * head, TILE * head + TILE)
            sums = by_distance(jnp.concatenate([before[rows], own[rows]], axis=1))
            others = jnp.sum(far[rows], keepdims=True)
            lane = lax.broadcasted_iota(jnp.int32, (1, 2 * TILE), 1)
            sums = sums + jnp.where(lane == FAR_LANE, others, 0.0)
            high = sums.astype(jnp.bfloat16).astype(jnp.float32)
            for step, part in enumerate((high, sums - high)):
                for half in range(2):
                    cell = part[:, TILE * half : TILE * half + TILE]
                    row = 4 * (2 * pair + head) + 2 * step + half
                    profile[pl.ds(row, 1), :] = cell
                    profile[pl.ds(row + 24, 1), :] = cell
        return carry

    lax.fori_loop(0, PAIRS, one_pair, 0)
    load_normed.wait()
    load_att.wait()
    pair_mixed = jnp.concatenate([d_mixed[0, :, core_rows(core)], d_mixed[1, :, core_rows(core)]])
    sums_ref[1, :, HALF:WIDTH] = plain_dot(att_t_ref[...], pair_mixed).astype(jnp.bfloat16)
    sums_ref[1, :, :HALF] = plain_dot(normed_t_ref[...], wide(dv_ref)).astype(jnp.bfloat16)
    cells = profile[...].astype(jnp.bfloat16)
    for step in range(WIDTH // 48):
        sums_ref[1, 48 * step : 48 * step + 48, WIDTH:] = cells
    saves[1].start()
    own_t = jnp.concatenate(
        [
            normed_t_ref[:, pl.ds(pl.multiple_of(tile_a * TILE, TILE), TILE)],
            normed_t_ref[:, pl.ds(pl.multiple_of(tile_b * TILE, TILE), TILE)],
        ],
        axis=1,
    )
    sums_ref[0, :, :HALF] = plain_dot(own_t, dq_ref[...]).astype(jnp.bfloat16)
    sums_ref[0, :, HALF:WIDTH] = plain_dot(normed_t_ref[...], wide(dk_ref)).astype(jnp.bfloat16)
    sums_ref[0, :, WIDTH:] = side_ref[...]
    saves[0].start()
    for pair in range(PAIRS):
        for copy in saves_of(pair):
            copy.wait()
    saves[1].wait()
    saves[0].wait()


def spread_kernel(
    place_ref,
    dq_ref,
    dk_any,
    dv_any,
    weights_any,
    kept_any,
    given_any,
    dk_ref,
    dv_ref,
    weights_ref,
    rows_ref,
    sems,
):
    tile_a, tile_b = own_tiles(place_ref)
    core = place_ref[1]
    chunks = 4
    size = ROWS // chunks
    loads = [
        pltpu.make_async_copy(weights_any.at[part], weights_ref.at[part], sems.at[part])
        for part in range(2)
    ]
    for chunk in range(chunks):
        at = pl.ds(size * chunk, size)
        for step, (from_any, to_ref) in enumerate(((dk_any, dk_ref), (dv_any, dv_ref))):
            loads.append(
                pltpu.make_async_copy(
                    from_any.at[:, at], to_ref.at[:, at], sems.at[2 + 2 * chunk + step]
                )
            )
    for load in loads:
        load.start()
    loads[0].wait()
    loads[1].wait()
    dqn = cols_dot(dq_ref[...], weights_ref[0, :, :HALF])

    def saves(chunk):
        copies = []
        for block in range(chunk * (size // 64), (chunk + 1) * (size // 64)):
            slab = block if block < 16 else 31 - block
            row = 0 if block < 16 else 64
            from_rows = rows_ref.at[pl.ds(64 * block, 64)]
            for to_any, wanted in (
                (kept_any, core == slab % 2),
                (given_any, core != slab % 2),
            ):
                copy = pltpu.make_async_copy(
                    from_rows, to_any.at[slab // 2, pl.ds(row, 64)], sems.at[10 + block]
                )
                copies.append((wanted, copy))
        return copies

    for chunk in range(chunks):
        at = slice(size * chunk, size * chunk + size)
        loads[2 + 2 * chunk].wait()
        loads[3 + 2 * chunk].wait()
        rows_ref[at, :] = (
            cols_dot(wide(dk_ref.at[:, at]), weights_ref[0, :, HALF:WIDTH])
            + cols_dot(wide(dv_ref.at[:, at]), weights_ref[1, :, :HALF])
        ).astype(jnp.bfloat16)
        for tile, rows in ((tile_a, slice(0, 128)), (tile_b, slice(128, 256))):

            @pl.when((tile >= chunk * size // TILE) & (tile < (chunk + 1) * size // TILE))
            def _():
                own = pl.ds(pl.multiple_of(tile * TILE, TILE), TILE)
                rows_ref[own, :] = (rows_ref[own, :].astype(jnp.float32) + dqn[rows]).astype(
                    jnp.bfloat16
                )

        for wanted, copy in saves(chunk):
            pl.when(wanted)(copy.start)
    for chunk in range(chunks):
        for wanted, copy in saves(chunk):
            pl.when(wanted)(copy.wait)


def up_kernel(place_ref, cot_ref, w_out_ref, up_ref):
    def one_block(block, carry):
        at = pl.ds(pl.multiple_of(block * 512, 512), 512)
        up_ref[at, :] = cols_dot(cot_ref[at, :], w_out_ref[...]).astype(jnp.bfloat16)
        return carry

    lax.fori_loop(0, cot_ref.shape[0] // 512, one_block, 0)


def expert_units(place_ref, rows_ref, partner_ref, up_ref, w_in_ref, side_ref, keep):
    block_rows = rows_ref.shape[0]
    lane = lax.broadcasted_iota(jnp.int32, (block_rows, 128), 1)
    rows = rows_ref[...]
    logits = plain_dot(rows, side_ref[...])
    partner = partner_ref[...].astype(jnp.float32)
    own = jnp.sum(jnp.where(lane == place_ref[2], logits, 0.0), axis=-1, keepdims=True)
    also = jnp.sum(
        jnp.where(lane.astype(jnp.float32) == partner, logits, 0.0), axis=-1, keepdims=True
    )
    top = jnp.maximum(own, also)
    own, also = jnp.exp(own - top), jnp.exp(also - top)
    gate = own / (own + also)
    for step in range(w_in_ref.shape[1] // 256):
        lanes = slice(256 * step, 256 * step + 256)
        value, slope = gelu_parts(plain_dot(rows, w_in_ref[:, lanes]))
        keep(lanes, value, gate, gate * up_ref[:, lanes].astype(jnp.float32) * slope)


def expert_kernel(
    place_ref,
    rows_ref,
    partner_ref,
    up_ref,
    w_in_ref,
    w_out_ref,
    side_ref,
    back_ref,
    inner,
    d_pre,
):
    def keep(lanes, value, gate, d_value):
        inner[:, lanes] = value.astype(jnp.bfloat16)
        d_pre[:, lanes] = d_value.astype(jnp.bfloat16)

    expert_units(place_ref, rows_ref, partner_ref, up_ref, w_in_ref, side_ref, keep)
    back_ref[:, :WIDTH] = plain_dot(inner[...], w_out_ref[...]).astype(jnp.bfloat16)
    back_ref[:, WIDTH:] = cols_dot(d_pre[...], w_in_ref[...]).astype(jnp.bfloat16)


def again_kernel(
    place_ref, rows_ref, partner_ref, up_ref, w_in_ref, side_ref, gated_ref, d_pre_ref
):
    def keep(lanes, value, gate, d_value):
        gated_ref[:, lanes] = (gate * value).astype(jnp.bfloat16)
        d_pre_ref[:, lanes] = d_value.astype(jnp.bfloat16)

    expert_units(place_ref, rows_ref, partner_ref, up_ref, w_in_ref, side_ref, keep)


def call(kernel, shapes, scratch, flops, place, *operands, anywhere=(), saved=0):
    outs = tuple(jax.ShapeDtypeStruct(shape, dtype) for shape, dtype in shapes)
    in_vmem, left = pl.BlockSpec(memory_space=pltpu.VMEM), pl.BlockSpec(memory_space=pl.ANY)
    specs = [left if at in anywhere else in_vmem for at in range(len(operands))]
    if place is not None:
        specs, operands = [pl.BlockSpec(memory_space=pltpu.SMEM)] + specs, (place, *operands)
    scratch = [pltpu.VMEM(shape, dtype) for shape, dtype in scratch]
    if anywhere:
        scratch.append(pltpu.SemaphoreType.DMA((48,)))
    return pl.pallas_call(
        kernel,
        out_shape=outs,
        in_specs=specs,
        out_specs=tuple(left if at < saved else in_vmem for at in range(len(outs))),
        scratch_shapes=scratch,
        compiler_params=pltpu.CompilerParams(vmem_limit_bytes=60 * 2**20),
        cost_estimate=pl.CostEstimate(
            flops=flops, bytes_accessed=16 * 2**20, transcendentals=3 * 10**6
        ),
    )(*operands)


ROWS = 16 * TILE


def near_biases(table):
    shapes = (((PAIRS, 2 * TILE, 2 * TILE), jnp.float32),)
    return call(near_kernel, shapes, (), 10**7, table)[0]


def attend(*operands):
    low, full = jnp.bfloat16, jnp.float32
    shapes = (
        ((ROWS, WIDTH), low),
        ((PAIRS, ROWS, 128), low),
        ((PAIRS, ROWS, 128), low),
        ((2 * TILE, HALF), low),
        ((2, TILE, HALF), low),
        ((4 * TILE, 128), full),
        ((WIDTH, 128), low),
    )
    scratch = (
        ((4 * TILE, ROWS), full),
        ((9, CHUNK, CHUNK), full),
        ((4 * TILE, 128), low),
        ((ROWS, WIDTH), low),
        ((2, WIDTH, SIDE_END), low),
        ((PAIRS, 2 * TILE, 2 * TILE), full),
        *shapes[:3],
    )
    return call(
        attend_kernel, shapes, scratch, 8 * 10**9, *operands, anywhere=(0, 1, 2, 3), saved=3
    )


def attend_back(*operands):
    low, full = jnp.bfloat16, jnp.float32
    shapes = (
        ((PAIRS, ROWS, 128), low),
        ((PAIRS, ROWS, 128), low),
        ((2, WIDTH, SIDE_END), low),
        ((2 * TILE, HALF), low),
    )
    scratch = (
        ((4 * TILE, ROWS), full),
        ((9, CHUNK, CHUNK), full),
        ((48, TILE), full),
        ((2, TILE, WIDTH), low),
        ((2 * TILE, HALF), low),
        ((4 * TILE, 128), low),
        ((4 * TILE, 128), low),
        ((4 * TILE, 1), full),
        ((4 * TILE, 1), full),
        ((128, 4 * TILE), low),
        ((128, 4 * TILE), low),
        ((128, ROWS), full),
        ((128, ROWS), full),
        ((PAIRS, ROWS, 128), low),
        ((PAIRS, ROWS, 128), low),
        ((PAIRS, 2 * TILE, 2 * TILE), full),
        ((WIDTH, ROWS), low),
        ((WIDTH, 2 * TILE), low),
        *shapes[:3],
    )
    return call(
        back_kernel, shapes, scratch, 12 * 10**9, *operands, anywhere=(1, 2, 7, 8, 9), saved=3
    )


def mid(rows, *operands):
    low, full = jnp.bfloat16, jnp.float32
    shapes = (((TILE, WIDTH), full), ((TILE, WIDTH), low), ((rows, WIDTH), low))
    return call(mid_kernel, shapes, (), 10**9, *operands)


def token_side(*operands):
    low, full = jnp.bfloat16, jnp.float32
    shapes = (
        ((TILE, WIDTH), low),
        ((TILE, WIDTH), full),
        ((TILE, WIDTH), low),
        ((WIDTH, 128), low),
    )
    return call(token_kernel, shapes, (), 10**9, None, *operands)


def up_pass(rows, hidden_units, *operands):
    (up,) = call(up_kernel, (((rows, hidden_units), jnp.bfloat16),), (), 3 * 10**9, *operands)
    return up


def spread(*operands):
    low = jnp.bfloat16
    shapes = (((8, TILE, WIDTH), low),) * 2
    scratch = (
        ((PAIRS, ROWS, 128), low),
        ((PAIRS, ROWS, 128), low),
        ((2, WIDTH, SIDE_END), low),
        ((ROWS, WIDTH), low),
    )
    return call(
        spread_kernel, shapes, scratch, 3 * 10**9, *operands, anywhere=(1, 2, 3), saved=2
    )


def by_rows(kernel, outs, scratch, flops, place, blocked, whole):
    count, block = blocked[0].shape[0], EXPERT_BLOCK
    low = jnp.bfloat16

    def spec(columns):
        return pl.BlockSpec((block, columns), lambda i: (i, 0))

    return pl.pallas_call(
        kernel,
        grid=(count // block,),
        out_shape=tuple(jax.ShapeDtypeStruct((count, columns), low) for columns in outs),
        in_specs=[
            pl.BlockSpec(memory_space=pltpu.SMEM),
            *(spec(array.shape[1]) for array in blocked),
            *(pl.BlockSpec(memory_space=pltpu.VMEM) for _ in whole),
        ],
        out_specs=tuple(spec(columns) for columns in outs),
        scratch_shapes=[pltpu.VMEM((block, columns), low) for columns in scratch],
        compiler_params=pltpu.CompilerParams(vmem_limit_bytes=EXPERT_VMEM),
        cost_estimate=pl.CostEstimate(
            flops=flops, bytes_accessed=20 * 2**20, transcendentals=2 * 10**6
        ),
    )(place, *blocked, *whole)


def expert_pass(place, rows, partner, up, w_in, w_out, side):
    units = w_in.shape[1]
    (back,) = by_rows(
        expert_kernel,
        (2 * WIDTH,),
        (units, units),
        8 * 10**9,
        place,
        (rows, partner, up),
        (w_in, w_out, side),
    )
    return back


def expert_again(place, rows, partner, up, w_in, side):
    units = w_in.shape[1]
    return by_rows(
        again_kernel, (units, units), (), 3 * 10**9, place, (rows, partner, up), (w_in, side)
    )


def swap(shard):
    return lax.ppermute(shard, CORE, [(0, 1), (1, 0)])


def to_all(shard, axes):
    devices = lax.axis_size(axes)
    return lax.all_to_all(
        jnp.broadcast_to(shard[None], (devices, *shard.shape)), axes, 0, 0, tiled=True
    )


def quad_exchange(blocks):
    me = lax.axis_index(QUAD)
    got = [lax.dynamic_index_in_dim(blocks, me, 0, keepdims=False)]
    for step in range(1, 4):
        part = lax.dynamic_index_in_dim(blocks, me ^ step, 0, keepdims=False)
        got.append(lax.ppermute(part, QUAD, [(i, i ^ step) for i in range(4)]))
    rows = []
    for place in range(4):
        row = got[0]
        for step in range(1, 4):
            row = jnp.where(me ^ step == place, got[step], row)
        rows.append(row)
    return jnp.stack(rows)


def exchange(blocks, axes):
    return lax.all_to_all(blocks, axes, split_axis=0, concat_axis=0, tiled=True)


def gelu_parts(pre):
    root = math.sqrt(2.0 / math.pi)
    square = pre * pre
    curve = jnp.tanh(pre * (root + (root * 0.044715) * square))
    share = 0.5 + 0.5 * curve
    value = pre * share
    slope = share + value * (1.0 - share) * (2 * root + (6 * root * 0.044715) * square)
    return value, slope


def shards(
    tokens,
    cotangent,
    routes,
    w_query,
    w_key,
    w_value,
    w_output,
    w_router,
    gain_attn,
    gain_ffn,
    bias_table,
    w_in,
    w_out,
):
    f32, bf16 = jnp.float32, jnp.bfloat16
    core = lax.axis_index(CORE)
    chip = lax.axis_index(CHIPS)
    expert = lax.axis_index(SEQ_CTX)
    on_first = core == 0
    tok_count, model_width = tokens.shape[1:]
    local_rows = w_query.shape[0]
    expert_count = w_router.shape[1]
    place = jnp.stack([chip, core, expert]).astype(jnp.int32)

    own_tokens = tokens[0]
    mine = to_all(own_tokens, CHIPS)
    other = swap(mine)

    quarters = jnp.stack([jnp.stack([w_query, w_key]), jnp.stack([w_value, w_output])])
    quarters = quarters.reshape(2, 2, local_rows, 2, HALF).transpose(3, 0, 2, 1, 4)
    quarters = quarters.reshape(2, 2, local_rows, 2 * HALF)
    extra = jnp.concatenate(
        [
            w_router,
            gain_attn[:, None],
            gain_ffn[:, None],
            jnp.zeros((local_rows, 128 - expert_count - 2), bf16),
        ],
        axis=1,
    )
    own_routes = routes.reshape(-1, 128).astype(bf16)
    own_routes = jnp.pad(own_routes, ((0, local_rows - own_routes.shape[0]), (0, 0)))
    extra = jnp.stack([extra, own_routes])
    extra = jnp.broadcast_to(extra[None], (2, *extra.shape))
    packed_weights = jnp.concatenate([quarters, extra], axis=-1).reshape(4, local_rows, -1)
    group_rows = 4 * local_rows
    weight_rows = quad_exchange(packed_weights).reshape(group_rows, -1)
    all_weights = to_all(weight_rows, SAME_CORE).reshape(2, model_width, -1)
    own_table = lax.dynamic_slice_in_dim(bias_table, core * (HEADS // 2), HEADS // 2, 1)
    near = near_biases(own_table)

    route_ids = routes[0]
    capacity = max(2, 2 * TOP * tok_count // expert_count)
    flat_ids = route_ids.reshape(-1)
    flat_marks = (flat_ids[:, None] == jnp.arange(expert_count, dtype=jnp.int32)).astype(jnp.int32)
    earlier = jnp.cumsum(flat_marks, axis=0, dtype=jnp.int32) - flat_marks
    slot_ids = jnp.sum(earlier * flat_marks, axis=-1, dtype=jnp.int32)
    row_index = (flat_ids * capacity + slot_ids).reshape(tok_count, TOP)
    exp_count = lax.axis_size("exp")
    device_count = expert_count * exp_count
    slots = jnp.arange(device_count * capacity, dtype=jnp.int32)
    slots = slots // (exp_count * capacity) * capacity + slots % capacity
    pick = (row_index.T[:, :, None] == slots[None, None, :]).astype(bf16)
    pack = (row_index.T[:, None, :] == slots[None, :, None]).astype(bf16)

    def to_experts(rows):
        return exchange(rows.reshape(device_count, capacity, -1), SEQ_CTX_EXP)

    cot_own = cotangent[0]
    all_pack = pack[0] + pack[1]
    cot_rows = plain_dot(all_pack, cot_own).astype(bf16)
    near, cot_rows, other, all_weights = lax.optimization_barrier(
        (near, cot_rows, other, all_weights)
    )
    cot_there = to_experts(cot_rows)
    wo_half = all_weights[1, :, HALF:model_width]
    wo_other = swap(wo_half)

    normed_all, keys, values, queries, attended, log_totals, side = attend(
        place, mine, other, all_weights, near
    )

    attended_other = swap(attended)
    pair_attended = jnp.concatenate(
        [
            jnp.where(on_first, attended, attended_other),
            jnp.where(on_first, attended_other, attended),
        ],
        axis=-1,
    )
    hidden, normed_ffn, packed = mid(
        device_count * capacity,
        place,
        attended,
        attended_other,
        own_tokens,
        side,
        wo_half,
        wo_other,
        all_pack,
    )
    there = to_experts(packed)

    inner_in, inner_out = w_in[0], w_out[0]
    flat_rows = there.reshape(-1, model_width)
    flat_cot = cot_there.reshape(flat_rows.shape[0], -1)
    all_routes = all_weights[1, :, model_width:].reshape(device_count, local_rows, 128)
    all_routes = all_routes[:, : TOP * tok_count // 128].reshape(device_count, -1)
    all_routes = all_routes.astype(jnp.int32)
    here = all_routes == expert
    rank = jnp.cumsum(here.astype(jnp.int32), axis=1, dtype=jnp.int32) - 1
    partners = jnp.flip(all_routes.reshape(device_count, -1, TOP), axis=2)
    partners = partners.reshape(device_count, 1, -1)
    in_slot = here[:, None, :] & (
        rank[:, None, :] == jnp.arange(capacity, dtype=jnp.int32)[None, :, None]
    )
    partner = jnp.sum(jnp.where(in_slot, partners, 0), axis=2, dtype=jnp.int32)
    partner = jnp.broadcast_to(partner.reshape(-1, 1), (device_count * capacity, 128)).astype(bf16)

    flat_cot, partner = lax.optimization_barrier((flat_cot, partner))
    up = up_pass(flat_rows.shape[0], inner_in.shape[1], place, flat_cot, inner_out)
    sent_back = expert_pass(place, flat_rows, partner, up, inner_in, inner_out, side)
    returned = exchange(sent_back.reshape(device_count, capacity, -1), SEQ_CTX_EXP)
    gated, d_pre = expert_again(place, flat_rows, partner, up, inner_in, side)
    grad_out_local = rows_dot(gated, flat_cot)
    grad_in_local = rows_dot(flat_rows, d_pre)
    normed_t = normed_all.T
    att_t = pair_attended.reshape(2 * tok_count, model_width).T

    returned, grad_out_local, grad_in_local, normed_t, att_t = lax.optimization_barrier(
        (returned, grad_out_local, grad_in_local, normed_t, att_t)
    )
    output, d_hidden, d_mixed, sums_side = token_side(
        returned.reshape(device_count * capacity, -1),
        pick.reshape(TOP * tok_count, -1),
        hidden,
        normed_ffn,
        cot_own,
        route_ids,
        side,
    )
    d_mixed_other = swap(d_mixed)

    d_keys, d_values, to_sum, d_queries = attend_back(
        place,
        queries,
        keys,
        values,
        attended,
        d_mixed,
        d_mixed_other,
        log_totals,
        near,
        normed_t,
        att_t,
        sums_side,
        wo_half,
        wo_other,
    )
    groups = model_width // group_rows
    to_add = exchange(to_sum.reshape(2 * groups, group_rows, -1), SAME_CORE)
    kept, given = spread(place, d_queries, d_keys, d_values, all_weights)
    chip_sums = (kept.astype(f32) + swap(given).astype(f32)).astype(bf16)
    to_add, chip_sums = lax.optimization_barrier((to_add, chip_sums))
    d_normed = jnp.sum(exchange(chip_sums, CHIPS).astype(f32), axis=0)
    summed = jnp.sum(to_add.astype(f32), axis=0)
    source = own_tokens.astype(f32)
    inv_first = lax.rsqrt(jnp.mean(source * source, axis=-1, keepdims=True) + epsilon)
    scaled_first = side[:, expert_count].astype(f32)[None, :] * d_normed
    grad_tokens = (
        d_hidden
        + inv_first * scaled_first
        - source * inv_first**3 * jnp.mean(scaled_first * source, axis=-1, keepdims=True)
    )

    cells = jnp.broadcast_to(
        summed[None, :, model_width:].reshape(1, 1, -1), (4, 1, 128 * group_rows)
    )
    cells = jnp.pad(cells, ((0, 0), (0, 0), (0, -cells.shape[2] % summed.shape[1])))
    finals = quad_exchange(
        jnp.concatenate(
            [summed.reshape(4, local_rows, -1), cells.reshape(4, -1, summed.shape[1])], axis=1
        )
    )
    finals = finals.reshape(2, 2, -1, summed.shape[1])
    body = finals[:, :, :local_rows]

    def both(part, begin):
        return jnp.concatenate(
            [body[0, part, :, begin : begin + HALF], body[1, part, :, begin : begin + HALF]], axis=1
        )

    grad_query, grad_key, grad_value, grad_output = both(0, 0), both(0, HALF), both(1, 0), both(1, HALF)
    grad_gain_attn = (
        jnp.sum(
            grad_query * w_query.astype(f32)
            + grad_key * w_key.astype(f32)
            + grad_value * w_value.astype(f32),
            axis=1,
        )
        / gain_attn.astype(f32)
    )
    last = body[0, 0, :, model_width:] + body[1, 0, :, model_width:]
    profile = finals[:, 1, local_rows:].reshape(2, -1)[:, : 128 * group_rows]
    profile = profile.reshape(HEADS, 2, 2 * TILE).sum(axis=1)
    far = (TILE - np.arange(2 * TILE)) % (2 * TILE)
    bucket = sum((far >= border).astype(np.int32) for border in limits())
    marks = (bucket[:, None] == np.arange(BUCKETS)).astype(np.float32)
    grad_table = lax.dot_general(
        jnp.asarray(marks), profile, (((0,), (1,)), ((), ())), precision=precise
    )
    return (
        output[None],
        grad_tokens[None],
        grad_query,
        grad_key,
        grad_value,
        grad_output,
        last[:, :expert_count],
        grad_gain_attn,
        last[:, expert_count],
        grad_table,
        grad_in_local[None],
        grad_out_local[None],
    )


def solution(mesh):
    split = Mesh(
        mesh.devices.reshape(mesh.shape["seq"], 2, 4, 2, mesh.shape["exp"]),
        ("seq", "ctx_0", "ctx_1", "ctx_2", "exp"),
    )
    in_specs = (
        P(("seq", "exp"), CTX, None),
        P(("seq", "exp"), CTX, None),
        P(("seq", "exp"), CTX, None),
        P(SEQ_CTX_EXP, None),
        P(SEQ_CTX_EXP, None),
        P(SEQ_CTX_EXP, None),
        P(SEQ_CTX_EXP, None),
        P(SEQ_CTX_EXP, None),
        P(SEQ_CTX_EXP),
        P(SEQ_CTX_EXP),
        P(),
        P(SEQ_CTX, None, "exp"),
        P(SEQ_CTX, "exp", None),
    )
    out_specs = (
        P(("seq", "exp"), CTX, None),
        P(("seq", "exp"), CTX, None),
        P(SEQ_CTX_EXP, None),
        P(SEQ_CTX_EXP, None),
        P(SEQ_CTX_EXP, None),
        P(SEQ_CTX_EXP, None),
        P(SEQ_CTX_EXP, None),
        P(SEQ_CTX_EXP),
        P(SEQ_CTX_EXP),
        P(),
        P(SEQ_CTX, None, "exp"),
        P(SEQ_CTX, "exp", None),
    )
    return jax.shard_map(
        shards, mesh=split, in_specs=in_specs, out_specs=out_specs, check_vma=False
    )
```

```python
import functools
import math

import jax
import jax.numpy as jnp
import numpy as np
from jax import lax
from jax.experimental import pallas as pl
from jax.experimental.pallas import tpu as pltpu
from jax.sharding import Mesh
from jax.sharding import PartitionSpec as P

HEADS = 12
HEAD = 64
TOP = 2
BUCKETS = 32
MAXDIST = 128
WIDTH = HEADS * HEAD
HALF = WIDTH // 2
PAIRS = HALF // 128
SIDE_GAIN = 64
SIDE_END = WIDTH + 128
FAR_LANE = 2 * 128 - 127
EXPERT_BLOCK = 256
EXPERT_VMEM = 60 * 2**20
TILE = 128
CHUNK = 256
CORE = "ctx_2"
CHIPS = ("ctx_0", "ctx_1")
SAME_CORE = ("exp", "seq", "ctx_0", "ctx_1")
QUAD = ("ctx_2", "exp")
SEQ_CTX_EXP = ("seq", "ctx_0", "ctx_1", "ctx_2", "exp")
CTX = ("ctx_0", "ctx_1", "ctx_2")
SEQ_CTX = ("seq", "ctx_0", "ctx_1", "ctx_2")
BLOCKED = -1000000000.0
epsilon = 1e-06
precise = lax.Precision.HIGHEST


def limits():
    exact_cut = BUCKETS // 2
    borders = []
    for bucket_step in range(1, BUCKETS):
        if bucket_step <= exact_cut:
            borders.append(bucket_step)
        else:
            borders.append(
                int(
                    math.ceil(
                        exact_cut * (MAXDIST / exact_cut) ** ((bucket_step - exact_cut) / exact_cut)
                    )
                )
            )
    return borders


def rows_dot(first_op, second_op):
    return lax.dot_general(
        first_op, second_op, (((0,), (0,)), ((), ())), preferred_element_type=jnp.float32
    )


def cols_dot(first_op, second_op):
    return lax.dot_general(
        first_op, second_op, (((1,), (1,)), ((), ())), preferred_element_type=jnp.float32
    )


def plain_dot(first_op, second_op):
    return jnp.dot(first_op, second_op, preferred_element_type=jnp.float32)


def own_tiles(place_ref):
    first = place_ref[0]
    return first, 15 - first


def fill_bias(bias_full, place_ref):
    tile_a, tile_b = own_tiles(place_ref)

    def fill(tile, carry):
        at = pl.ds(pl.multiple_of(tile * TILE, TILE), TILE)
        bias_full[0:256, at] = jnp.full((256, TILE), jnp.where(tile <= tile_a, 0.0, BLOCKED))
        bias_full[256:512, at] = jnp.full((256, TILE), jnp.where(tile <= tile_b, 0.0, BLOCKED))
        return carry

    lax.fori_loop(0, 16, fill, 0)


def near_kernel(table_ref, near_ref):
    row = lax.broadcasted_iota(jnp.int32, (TILE, 2 * TILE), 0)
    column = lax.broadcasted_iota(jnp.int32, (TILE, 2 * TILE), 1)
    distance = row + TILE - column
    for head in range(2 * PAIRS):
        last = table_ref[BUCKETS - 1, head]
        bias = jnp.full(distance.shape, table_ref[0, head] - last)
        for bucket, border in enumerate(limits()):
            bias = jnp.where(distance >= border, table_ref[bucket + 1, head] - last, bias)
        rows = slice(TILE * (head % 2), TILE * (head % 2) + TILE)
        near_ref[head // 2, rows, :] = jnp.where(distance >= 0, bias, BLOCKED)


def near_bias(bias_full, near_ref, place_ref, pair):
    tile_a, tile_b = own_tiles(place_ref)
    for rows, tile in ((slice(0, 256), tile_a), (slice(256, 512), tile_b)):
        bias_full[rows, pl.ds(pl.multiple_of(tile * TILE, TILE), TILE)] = near_ref[pair, :, TILE:]

        @pl.when(tile > 0)
        def _():
            before = pl.ds(pl.multiple_of((tile - 1) * TILE, TILE), TILE)
            bias_full[rows, before] = near_ref[pair, :, :TILE]


def by_head(rows):
    left = lax.broadcasted_iota(jnp.int32, (TILE, TILE), 1) < HEAD
    rows = rows.astype(jnp.float32)
    parts = []
    for tile in (rows[:TILE], rows[TILE:]):
        parts.append(jnp.where(left, tile, 0.0))
        parts.append(jnp.where(left, 0.0, tile))
    return jnp.concatenate(parts, axis=0)


def side_by_side(four):
    left = lax.broadcasted_iota(jnp.int32, (TILE, TILE), 1) < HEAD
    return (
        jnp.where(left, four[:TILE], four[TILE : 2 * TILE]),
        jnp.where(left, four[2 * TILE : 3 * TILE], four[3 * TILE :]),
    )


def later_units(tile_a):
    reach = tile_a // 2
    units = []
    for step in range(1, 4):
        of_first = step <= reach
        chunk = jnp.where(of_first, step, 4 + step - reach)
        units.append((of_first, jnp.where(of_first, 0, 256), chunk))
    return units


def chunk_at(chunk):
    return pl.ds(pl.multiple_of(chunk * CHUNK, CHUNK), CHUNK)


def row_at(first):
    return pl.ds(pl.multiple_of(first, 256), 256)


def pair_lanes(pair):
    return pl.ds(pl.multiple_of(pair * 128, 128), 128)


def side_row(side, lane):
    return jnp.concatenate(
        [
            jnp.transpose(side[128 * step : 128 * step + 128].astype(jnp.float32))[lane : lane + 1]
            for step in range(WIDTH // 128)
        ],
        axis=1,
    )


def attend_kernel(
    place_ref,
    mine_any,
    other_any,
    weights_any,
    near_any,
    normed_any,
    k_any,
    v_any,
    q_ref,
    att_ref,
    lse_ref,
    side_ref,
    bias_full,
    scores,
    query,
    tokens,
    weights_ref,
    near_ref,
    normed_ref,
    k_ref,
    v_ref,
    sems,
):
    load_first = pltpu.make_async_copy(weights_any.at[0], weights_ref.at[0], sems.at[0])
    load_second = pltpu.make_async_copy(weights_any.at[1], weights_ref.at[1], sems.at[1])
    load_near = pltpu.make_async_copy(near_any, near_ref, sems.at[4])
    save_normed = pltpu.make_async_copy(normed_ref, normed_any, sems.at[5])
    save_k = pltpu.make_async_copy(k_ref, k_any, sems.at[6])
    save_v = pltpu.make_async_copy(v_ref, v_any, sems.at[7])
    tile_a, tile_b = own_tiles(place_ref)
    core = place_ref[1]

    def load_tokens(block):
        slab = block if block < 16 else 31 - block
        chip, row = slab // 2, 0 if block < 16 else 64
        copies = []
        for which, (from_any, from_core) in enumerate(((mine_any, core), (other_any, 1 - core))):
            to_block = 2 * chip + from_core if block < 16 else 31 - 2 * chip - from_core
            copies.append(
                pltpu.make_async_copy(
                    from_any.at[chip, row : row + 64],
                    tokens.at[pl.ds(pl.multiple_of(to_block * 64, 64), 64)],
                    sems.at[8 + block // 2 * 2 + which],
                )
            )
        return copies

    load_first.start()
    for block in range(0, 8, 2):
        for copy in load_tokens(block):
            copy.start()
    load_second.start()
    for block in range(8, 32, 2):
        for copy in load_tokens(block):
            copy.start()
    load_near.start()
    fill_bias(bias_full, place_ref)
    load_first.wait()
    side_ref[...] = weights_ref[0, :, WIDTH:]
    gain = side_row(side_ref[...], SIDE_GAIN)

    def norm_part(part):
        for block in range(8 * part, 8 * part + 8, 2):
            for copy in load_tokens(block):
                copy.wait()
            at = slice(64 * block, 64 * block + 128)
            source = tokens[at, :].astype(jnp.float32)
            inv = lax.rsqrt(jnp.mean(source * source, axis=-1, keepdims=True) + epsilon)
            normed_ref[at, :] = (source * inv * gain).astype(jnp.bfloat16)

    norm_part(0)
    load_second.wait()
    for part in range(4):
        if part < 3:
            norm_part(part + 1)
        at = slice(512 * part, 512 * part + 512)
        rows = normed_ref[at, :]
        for to_ref, weight in (
            (k_ref, weights_ref[0, :, HALF:WIDTH]),
            (v_ref, weights_ref[1, :, :HALF]),
        ):
            product = plain_dot(rows, weight).astype(jnp.bfloat16)
            for pair in range(PAIRS):
                to_ref[pair, at, :] = product[:, 128 * pair : 128 * pair + 128]
    save_normed.start()
    save_k.start()
    save_v.start()
    own = jnp.concatenate(
        [
            normed_ref[pl.ds(pl.multiple_of(tile_a * TILE, TILE), TILE), :],
            normed_ref[pl.ds(pl.multiple_of(tile_b * TILE, TILE), TILE), :],
        ],
        axis=0,
    )
    q_ref[...] = plain_dot(own, weights_ref[0, :, :HALF]).astype(jnp.bfloat16)
    load_near.wait()
    units = later_units(tile_a)
    lse_ref[...] = jnp.zeros_like(lse_ref)

    def one_pair(pair, carry):
        near_bias(bias_full, near_ref, place_ref, pair)
        lanes = pair_lanes(pair)
        query[...] = (by_head(q_ref[:, lanes]) * HEAD**-0.5).astype(jnp.bfloat16)

        def widest(part):
            return jnp.maximum(part[:, :128], part[:, 128:])

        both = cols_dot(query[...], k_ref[pair, 0:CHUNK, :]) + bias_full[:, 0:CHUNK]
        scores[0], scores[4] = both[:256], both[256:]
        top_a, top_b = widest(both[:256]), widest(both[256:])
        for chunk in range(1, 5):
            at = slice(chunk * CHUNK, (chunk + 1) * CHUNK)
            part = cols_dot(query[256:512, :], k_ref[pair, at, :]) + bias_full[256:512, at]
            scores[4 + chunk] = part
            top_b = jnp.maximum(top_b, widest(part))
        for step, (of_first, first, chunk) in enumerate(units):
            part = (
                cols_dot(query[row_at(first), :], k_ref[pair, chunk_at(chunk), :])
                + bias_full[row_at(first), chunk_at(chunk)]
            )
            scores[1 + step] = part
            here = widest(part)
            top_a = jnp.maximum(top_a, jnp.where(of_first, here, 2 * BLOCKED))
            top_b = jnp.maximum(top_b, jnp.where(of_first, 2 * BLOCKED, here))
        top_a = jnp.max(top_a, axis=-1, keepdims=True)
        top_b = jnp.max(top_b, axis=-1, keepdims=True)

        def raise_to(part, top, at):
            raised = jnp.exp(part - top)
            return raised[:, :128] + raised[:, 128:], plain_dot(
                raised.astype(jnp.bfloat16), v_ref[pair, at, :]
            )

        total_a, merged_a = raise_to(scores[0], top_a, slice(0, CHUNK))
        total_b, merged_b = raise_to(scores[4], top_b, slice(0, CHUNK))
        for chunk in range(1, 5):
            here, product = raise_to(
                scores[4 + chunk], top_b, slice(chunk * CHUNK, (chunk + 1) * CHUNK)
            )
            total_b, merged_b = total_b + here, merged_b + product
        for step, (of_first, first, chunk) in enumerate(units):
            top = jnp.where(of_first, top_a, top_b)
            here, product = raise_to(scores[1 + step], top, chunk_at(chunk))
            total_a = total_a + jnp.where(of_first, here, 0.0)
            total_b = total_b + jnp.where(of_first, 0.0, here)
            merged_a = merged_a + jnp.where(of_first, product, 0.0)
            merged_b = merged_b + jnp.where(of_first, 0.0, product)
        total_a = jnp.sum(total_a, axis=-1, keepdims=True)
        total_b = jnp.sum(total_b, axis=-1, keepdims=True)
        lane = lax.broadcasted_iota(jnp.int32, (2 * TILE, 128), 1)
        for rows, lse in (
            (slice(0, 256), top_a + jnp.log(total_a)),
            (slice(256, 512), top_b + jnp.log(total_b)),
        ):
            lse_ref[rows, :] = jnp.where(lane == pair, lse, lse_ref[rows, :])
        first, second = side_by_side(
            jnp.concatenate([merged_a / total_a, merged_b / total_b], axis=0)
        )
        first, second = first.astype(jnp.bfloat16), second.astype(jnp.bfloat16)
        att_ref[0, 0:64, lanes] = first[:64]
        att_ref[1, 0:64, lanes] = first[64:]
        att_ref[1, 64:128, lanes] = second[:64]
        att_ref[0, 64:128, lanes] = second[64:]
        return carry

    lax.fori_loop(0, PAIRS, one_pair, 0)
    save_normed.wait()
    save_k.wait()
    save_v.wait()


def core_rows(core):
    return pl.ds(pl.multiple_of(core * HALF, 128), HALF)


def mid_kernel(
    place_ref,
    mine_ref,
    other_ref,
    tokens_ref,
    side_ref,
    wo_mine_ref,
    wo_other_ref,
    pack_ref,
    hidden_ref,
    normed_ref,
    packed_ref,
):
    core = place_ref[1]
    mine, other = mine_ref[core], other_ref[core]
    mine_rows, other_rows = core_rows(core), core_rows(1 - core)
    hidden_ref[:, mine_rows] = plain_dot(
        mine, wo_mine_ref[mine_rows, :]
    ) + plain_dot(other, wo_mine_ref[other_rows, :])
    hidden_ref[:, other_rows] = plain_dot(mine, wo_other_ref[mine_rows, :]) + plain_dot(
        other, wo_other_ref[other_rows, :]
    )
    hidden = tokens_ref[...].astype(jnp.float32) + hidden_ref[...]
    hidden_ref[...] = hidden
    inv = lax.rsqrt(jnp.mean(hidden * hidden, axis=-1, keepdims=True) + epsilon)
    normed = (hidden * inv * side_row(side_ref[...], SIDE_GAIN + 1)).astype(jnp.bfloat16)
    normed_ref[...] = normed
    packed_ref[...] = plain_dot(pack_ref[...], normed).astype(jnp.bfloat16)


def token_kernel(
    back_ref,
    pick_ref,
    hidden_ref,
    normed_ref,
    cot_ref,
    routes_ref,
    side_ref,
    out_ref,
    d_hidden_ref,
    d_mixed_ref,
    sums_ref,
):
    picked = plain_dot(pick_ref[...], back_ref[...])
    side = side_ref[...]
    logits = plain_dot(normed_ref[...], side)
    lane = lax.broadcasted_iota(jnp.int32, (TILE, 128), 1)
    routes = routes_ref[...]
    marks = [lane == routes[:, k : k + 1] for k in range(TOP)]
    chosen = [jnp.sum(jnp.where(mark, logits, 0.0), axis=-1, keepdims=True) for mark in marks]
    top = jnp.maximum(*chosen)
    raised = [jnp.exp(one - top) for one in chosen]
    gates = [one / (raised[0] + raised[1]) for one in raised]
    rows = [
        picked[TILE * k : TILE * k + TILE, :WIDTH].astype(jnp.bfloat16).astype(jnp.float32)
        for k in range(TOP)
    ]
    hidden = hidden_ref[...]
    out_ref[...] = (hidden + (gates[0] * rows[0] + gates[1] * rows[1])).astype(jnp.bfloat16)
    grad_top = cot_ref[...].astype(jnp.float32)
    d_gates = [jnp.sum(grad_top * one, axis=-1, keepdims=True) for one in rows]
    mean_gate = gates[0] * d_gates[0] + gates[1] * d_gates[1]
    d_logits = sum(
        jnp.where(mark, gate * (d_gate - mean_gate), 0.0)
        for mark, gate, d_gate in zip(marks, gates, d_gates)
    ).astype(jnp.bfloat16)
    d_normed = picked[:TILE, WIDTH:] + picked[TILE:, WIDTH:] + cols_dot(d_logits, side)
    inv = lax.rsqrt(jnp.mean(hidden * hidden, axis=-1, keepdims=True) + epsilon)
    scaled = side_row(side, SIDE_GAIN + 1) * d_normed
    d_hidden = (
        grad_top
        + inv * scaled
        - hidden * (inv * inv * inv) * jnp.mean(scaled * hidden, axis=-1, keepdims=True)
    )
    d_hidden_ref[...] = d_hidden
    d_mixed_ref[...] = d_hidden.astype(jnp.bfloat16)
    d_gain = jnp.sum(d_normed * hidden * inv, axis=0, keepdims=True)
    d_router = rows_dot(normed_ref[...], d_logits)
    for step in range(WIDTH // 128):
        at = slice(128 * step, 128 * step + 128)
        column = jnp.transpose(jnp.broadcast_to(d_gain[:, at], (128, 128)))
        sums_ref[at, :] = jnp.where(lane == SIDE_GAIN, column, d_router[at]).astype(jnp.bfloat16)


def tile_order(ref, lanes):
    return jnp.concatenate(
        [ref[0, 0:64, lanes], ref[1, 0:64, lanes], ref[1, 64:128, lanes], ref[0, 64:128, lanes]],
        axis=0,
    )


def by_distance(tiles):
    for half in (64, 32, 16, 8):
        tiles = tiles[:half] + pltpu.roll(tiles[half:], 2 * TILE - half, 1)
    row = lax.broadcasted_iota(jnp.int32, tiles.shape, 0)
    for step in (4, 2, 1):
        moved = pltpu.roll(tiles, 2 * TILE - step, 1)
        tiles = jnp.where((row & step) != 0, moved, tiles)
    return jnp.sum(tiles, axis=0, keepdims=True)


def wide(ref):
    return jnp.concatenate([ref[pair] for pair in range(PAIRS)], axis=1)


def back_kernel(
    place_ref,
    q_any,
    k_any,
    v_any,
    att_any,
    mixed_any,
    mixed_other_any,
    lse_any,
    near_any,
    normed_t_any,
    att_t_any,
    side_any,
    wo_mine_any,
    wo_other_any,
    dk_any,
    dv_any,
    sums_any,
    dq_ref,
    bias_full,
    d_scores,
    profile,
    d_mixed,
    d_att,
    query,
    grads,
    row_dots,
    row_lse,
    query_t,
    grads_t,
    dk_t,
    dv_t,
    k_ref,
    v_ref,
    near_ref,
    normed_t_ref,
    att_t_ref,
    dk_ref,
    dv_ref,
    sums_ref,
    q_ref,
    att_ref,
    lse_ref,
    side_ref,
    wo_mine_ref,
    wo_other_ref,
    sems,
):
    load_normed = pltpu.make_async_copy(normed_t_any, normed_t_ref, sems.at[0])
    load_att = pltpu.make_async_copy(att_t_any, att_t_ref, sems.at[1])
    def saves_of(pair):
        return [
            pltpu.make_async_copy(dk_ref.at[pair], dk_any.at[pair], sems.at[20 + 2 * pair]),
            pltpu.make_async_copy(dv_ref.at[pair], dv_any.at[pair], sems.at[21 + 2 * pair]),
        ]

    def loads_of(pair):
        return [
            pltpu.make_async_copy(from_any.at[pair], to_ref.at[pair], sems.at[8 + 4 * step + pair])
            for step, (from_any, to_ref) in enumerate(
                ((k_any, k_ref), (v_any, v_ref), (near_any, near_ref))
            )
        ]

    saves = [
        pltpu.make_async_copy(sums_ref.at[part], sums_any.at[part], sems.at[4 + part])
        for part in range(2)
    ]
    core = place_ref[1]
    first = [
        pltpu.make_async_copy(from_any, to_ref, sems.at[26 + step])
        for step, (from_any, to_ref) in enumerate(
            (
                (mixed_any, d_mixed.at[core]),
                (mixed_other_any, d_mixed.at[1 - core]),
                (wo_mine_any, wo_mine_ref),
                (wo_other_any, wo_other_ref),
            )
        )
    ]
    second = [
        pltpu.make_async_copy(from_any, to_ref, sems.at[30 + step])
        for step, (from_any, to_ref) in enumerate(
            ((q_any, q_ref), (att_any, att_ref), (lse_any, lse_ref), (side_any, side_ref))
        )
    ]
    for load in (*first, *second):
        load.start()
    for pair in range(PAIRS):
        for load in loads_of(pair):
            load.start()
    load_normed.start()
    load_att.start()
    tile_a, tile_b = own_tiles(place_ref)
    fill_bias(bias_full, place_ref)
    for load in first:
        load.wait()
    d_att[...] = (
        cols_dot(tile_order(d_mixed, core_rows(core)), wo_mine_ref[core_rows(core), :])
        + cols_dot(tile_order(d_mixed, core_rows(1 - core)), wo_other_ref[core_rows(core), :])
    ).astype(jnp.bfloat16)
    for load in second:
        load.wait()
    units = later_units(tile_a)
    reach = tile_a // 2

    def one_pair(pair, carry):
        for load in loads_of(pair):
            load.wait()
        near_bias(bias_full, near_ref, place_ref, pair)
        lanes = pair_lanes(pair)
        query[...] = (by_head(q_ref[:, lanes]) * HEAD**-0.5).astype(jnp.bfloat16)
        some = by_head(d_att[:, lanes])
        outs = by_head(tile_order(att_ref, lanes))
        row_dots[...] = jnp.sum(some * outs, axis=-1, keepdims=True)
        grads[...] = some.astype(jnp.bfloat16)
        lane = lax.broadcasted_iota(jnp.int32, (4 * TILE, 128), 1)
        row_lse[...] = jnp.sum(jnp.where(lane == pair, lse_ref[...], 0.0), axis=-1, keepdims=True)
        rest = slice(5 * CHUNK, 8 * CHUNK)
        dk_t[:, rest] = jnp.zeros((128, 3 * CHUNK), jnp.float32)
        dv_t[:, rest] = jnp.zeros((128, 3 * CHUNK), jnp.float32)
        query_t[...] = jnp.transpose(query[...])
        grads_t[...] = jnp.transpose(grads[...])

        def unit(rows, at):
            keys = k_ref[pair, at, :]
            probs = jnp.exp(
                cols_dot(query[rows, :], keys) + bias_full[rows, at] - row_lse[rows, :]
            )
            d_part = probs * (cols_dot(grads[rows, :], v_ref[pair, at, :]) - row_dots[rows, :])
            low = d_part.astype(jnp.bfloat16)
            d_values = plain_dot(grads_t[:, rows], probs.astype(jnp.bfloat16))
            d_keys = plain_dot(query_t[:, rows], low)
            return d_part, plain_dot(low, keys), d_keys, d_values

        both, dq, d_keys, d_values = unit(slice(0, 512), slice(0, CHUNK))
        d_scores[0], d_scores[4] = both[:256], both[256:]
        dk_t[:, 0:CHUNK] = d_keys
        dv_t[:, 0:CHUNK] = d_values
        dq_a, dq_b = dq[:256], dq[256:]
        total = (both[:256, :128] + both[:256, 128:]) + (both[256:, :128] + both[256:, 128:])
        for chunk in range(1, 5):
            at = slice(chunk * CHUNK, (chunk + 1) * CHUNK)
            part, dq, d_keys, d_values = unit(slice(256, 512), at)
            d_scores[4 + chunk] = part
            dk_t[:, at] = d_keys
            dv_t[:, at] = d_values
            dq_b = dq_b + dq
            total = total + (part[:, :128] + part[:, 128:])
        for step, (of_first, first, chunk) in enumerate(units):
            at = chunk_at(chunk)
            part, dq, d_keys, d_values = unit(row_at(first), at)
            d_scores[1 + step] = part
            dk_t[:, at] = dk_t[:, at] + d_keys
            dv_t[:, at] = dv_t[:, at] + d_values
            dq_a = dq_a + jnp.where(of_first, dq, 0.0)
            dq_b = dq_b + jnp.where(of_first, 0.0, dq)
            total = total + (part[:, :128] + part[:, 128:])
        dk_ref[pair] = jnp.transpose(dk_t[...].astype(jnp.bfloat16))
        dv_ref[pair] = jnp.transpose(dv_t[...].astype(jnp.bfloat16))
        for copy in saves_of(pair):
            copy.start()
        first, second = side_by_side(jnp.concatenate([dq_a, dq_b], axis=0) * HEAD**-0.5)
        dq_ref[0:128, lanes] = first.astype(jnp.bfloat16)
        dq_ref[128:256, lanes] = second.astype(jnp.bfloat16)

        def tile_of(slot, tile):
            return d_scores[slot, :, pl.ds(pl.multiple_of(tile % 2 * TILE, TILE), TILE)]

        def slot_b(tile):
            chunk = tile // 2
            return jnp.where(chunk <= 4, 4 + chunk, chunk - 4 + reach)

        own = tile_of(reach, tile_a) + tile_of(slot_b(tile_b), tile_b)
        ahead = jnp.maximum(tile_a - 1, 0)
        before = tile_of(slot_b(tile_b - 1), tile_b - 1) + jnp.where(
            tile_a > 0, tile_of(ahead // 2, ahead), 0.0
        )
        far = total - own - before
        for head in range(2):
            rows = slice(TILE * head, TILE * head + TILE)
            sums = by_distance(jnp.concatenate([before[rows], own[rows]], axis=1))
            others = jnp.sum(far[rows], keepdims=True)
            lane = lax.broadcasted_iota(jnp.int32, (1, 2 * TILE), 1)
            sums = sums + jnp.where(lane == FAR_LANE, others, 0.0)
            high = sums.astype(jnp.bfloat16).astype(jnp.float32)
            for step, part in enumerate((high, sums - high)):
                for half in range(2):
                    cell = part[:, TILE * half : TILE * half + TILE]
                    row = 4 * (2 * pair + head) + 2 * step + half
                    profile[pl.ds(row, 1), :] = cell
                    profile[pl.ds(row + 24, 1), :] = cell
        return carry

    lax.fori_loop(0, PAIRS, one_pair, 0)
    load_normed.wait()
    load_att.wait()
    pair_mixed = jnp.concatenate([d_mixed[0, :, core_rows(core)], d_mixed[1, :, core_rows(core)]])
    sums_ref[1, :, HALF:WIDTH] = plain_dot(att_t_ref[...], pair_mixed).astype(jnp.bfloat16)
    sums_ref[1, :, :HALF] = plain_dot(normed_t_ref[...], wide(dv_ref)).astype(jnp.bfloat16)
    cells = profile[...].astype(jnp.bfloat16)
    for step in range(WIDTH // 48):
        sums_ref[1, 48 * step : 48 * step + 48, WIDTH:] = cells
    saves[1].start()
    own_t = jnp.concatenate(
        [
            normed_t_ref[:, pl.ds(pl.multiple_of(tile_a * TILE, TILE), TILE)],
            normed_t_ref[:, pl.ds(pl.multiple_of(tile_b * TILE, TILE), TILE)],
        ],
        axis=1,
    )
    sums_ref[0, :, :HALF] = plain_dot(own_t, dq_ref[...]).astype(jnp.bfloat16)
    sums_ref[0, :, HALF:WIDTH] = plain_dot(normed_t_ref[...], wide(dk_ref)).astype(jnp.bfloat16)
    sums_ref[0, :, WIDTH:] = side_ref[...]
    saves[0].start()
    for pair in range(PAIRS):
        for copy in saves_of(pair):
            copy.wait()
    saves[1].wait()
    saves[0].wait()


def spread_kernel(
    place_ref,
    dq_ref,
    dk_any,
    dv_any,
    weights_any,
    kept_any,
    given_any,
    dk_ref,
    dv_ref,
    weights_ref,
    rows_ref,
    sems,
):
    tile_a, tile_b = own_tiles(place_ref)
    core = place_ref[1]
    chunks = 4
    size = ROWS // chunks
    loads = [
        pltpu.make_async_copy(weights_any.at[part], weights_ref.at[part], sems.at[part])
        for part in range(2)
    ]
    for chunk in range(chunks):
        at = pl.ds(size * chunk, size)
        for step, (from_any, to_ref) in enumerate(((dk_any, dk_ref), (dv_any, dv_ref))):
            loads.append(
                pltpu.make_async_copy(
                    from_any.at[:, at], to_ref.at[:, at], sems.at[2 + 2 * chunk + step]
                )
            )
    for load in loads:
        load.start()
    loads[0].wait()
    loads[1].wait()
    dqn = cols_dot(dq_ref[...], weights_ref[0, :, :HALF])

    def saves(chunk):
        copies = []
        for block in range(chunk * (size // 64), (chunk + 1) * (size // 64)):
            slab = block if block < 16 else 31 - block
            row = 0 if block < 16 else 64
            from_rows = rows_ref.at[pl.ds(64 * block, 64)]
            for to_any, wanted in (
                (kept_any, core == slab % 2),
                (given_any, core != slab % 2),
            ):
                copy = pltpu.make_async_copy(
                    from_rows, to_any.at[slab // 2, pl.ds(row, 64)], sems.at[10 + block]
                )
                copies.append((wanted, copy))
        return copies

    for chunk in range(chunks):
        at = slice(size * chunk, size * chunk + size)
        loads[2 + 2 * chunk].wait()
        loads[3 + 2 * chunk].wait()
        rows_ref[at, :] = (
            cols_dot(wide(dk_ref.at[:, at]), weights_ref[0, :, HALF:WIDTH])
            + cols_dot(wide(dv_ref.at[:, at]), weights_ref[1, :, :HALF])
        ).astype(jnp.bfloat16)
        for tile, rows in ((tile_a, slice(0, 128)), (tile_b, slice(128, 256))):

            @pl.when((tile >= chunk * size // TILE) & (tile < (chunk + 1) * size // TILE))
            def _():
                own = pl.ds(pl.multiple_of(tile * TILE, TILE), TILE)
                rows_ref[own, :] = (rows_ref[own, :].astype(jnp.float32) + dqn[rows]).astype(
                    jnp.bfloat16
                )

        for wanted, copy in saves(chunk):
            pl.when(wanted)(copy.start)
    for chunk in range(chunks):
        for wanted, copy in saves(chunk):
            pl.when(wanted)(copy.wait)


def up_kernel(place_ref, cot_ref, w_out_ref, up_ref):
    def one_block(block, carry):
        at = pl.ds(pl.multiple_of(block * 512, 512), 512)
        up_ref[at, :] = cols_dot(cot_ref[at, :], w_out_ref[...]).astype(jnp.bfloat16)
        return carry

    lax.fori_loop(0, cot_ref.shape[0] // 512, one_block, 0)


def expert_units(place_ref, rows_ref, partner_ref, up_ref, w_in_ref, side_ref, keep):
    block_rows = rows_ref.shape[0]
    lane = lax.broadcasted_iota(jnp.int32, (block_rows, 128), 1)
    rows = rows_ref[...]
    logits = plain_dot(rows, side_ref[...])
    partner = partner_ref[...].astype(jnp.float32)
    own = jnp.sum(jnp.where(lane == place_ref[2], logits, 0.0), axis=-1, keepdims=True)
    also = jnp.sum(
        jnp.where(lane.astype(jnp.float32) == partner, logits, 0.0), axis=-1, keepdims=True
    )
    top = jnp.maximum(own, also)
    own, also = jnp.exp(own - top), jnp.exp(also - top)
    gate = own / (own + also)
    for step in range(w_in_ref.shape[1] // 256):
        lanes = slice(256 * step, 256 * step + 256)
        value, slope = gelu_parts(plain_dot(rows, w_in_ref[:, lanes]))
        keep(lanes, value, gate, up_ref[:, lanes].astype(jnp.float32) * slope)
    return gate


def expert_kernel(
    place_ref,
    rows_ref,
    partner_ref,
    up_ref,
    w_in_ref,
    w_out_ref,
    side_ref,
    back_ref,
    inner,
    d_pre,
):
    def keep(lanes, value, gate, d_value):
        inner[:, lanes] = value.astype(jnp.bfloat16)
        d_pre[:, lanes] = d_value.astype(jnp.bfloat16)

    gate = expert_units(place_ref, rows_ref, partner_ref, up_ref, w_in_ref, side_ref, keep)
    back_ref[:, :WIDTH] = plain_dot(inner[...], w_out_ref[...]).astype(jnp.bfloat16)
    back_ref[:, WIDTH:] = (gate * cols_dot(d_pre[...], w_in_ref[...])).astype(jnp.bfloat16)


def again_kernel(
    place_ref, rows_ref, partner_ref, up_ref, w_in_ref, side_ref, gated_ref, d_pre_ref
):
    def keep(lanes, value, gate, d_value):
        gated_ref[:, lanes] = (gate * value).astype(jnp.bfloat16)
        d_pre_ref[:, lanes] = (gate * d_value).astype(jnp.bfloat16)

    expert_units(place_ref, rows_ref, partner_ref, up_ref, w_in_ref, side_ref, keep)


def call(kernel, shapes, scratch, flops, place, *operands, anywhere=(), saved=0):
    outs = tuple(jax.ShapeDtypeStruct(shape, dtype) for shape, dtype in shapes)
    in_vmem, left = pl.BlockSpec(memory_space=pltpu.VMEM), pl.BlockSpec(memory_space=pl.ANY)
    specs = [left if at in anywhere else in_vmem for at in range(len(operands))]
    if place is not None:
        specs, operands = [pl.BlockSpec(memory_space=pltpu.SMEM)] + specs, (place, *operands)
    scratch = [pltpu.VMEM(shape, dtype) for shape, dtype in scratch]
    if anywhere:
        scratch.append(pltpu.SemaphoreType.DMA((48,)))
    return pl.pallas_call(
        kernel,
        out_shape=outs,
        in_specs=specs,
        out_specs=tuple(left if at < saved else in_vmem for at in range(len(outs))),
        scratch_shapes=scratch,
        compiler_params=pltpu.CompilerParams(vmem_limit_bytes=60 * 2**20),
        cost_estimate=pl.CostEstimate(
            flops=flops, bytes_accessed=16 * 2**20, transcendentals=3 * 10**6
        ),
    )(*operands)


ROWS = 16 * TILE


def near_biases(table):
    shapes = (((PAIRS, 2 * TILE, 2 * TILE), jnp.float32),)
    return call(near_kernel, shapes, (), 10**7, table)[0]


def attend(*operands):
    low, full = jnp.bfloat16, jnp.float32
    shapes = (
        ((ROWS, WIDTH), low),
        ((PAIRS, ROWS, 128), low),
        ((PAIRS, ROWS, 128), low),
        ((2 * TILE, HALF), low),
        ((2, TILE, HALF), low),
        ((4 * TILE, 128), full),
        ((WIDTH, 128), low),
    )
    scratch = (
        ((4 * TILE, ROWS), full),
        ((9, CHUNK, CHUNK), full),
        ((4 * TILE, 128), low),
        ((ROWS, WIDTH), low),
        ((2, WIDTH, SIDE_END), low),
        ((PAIRS, 2 * TILE, 2 * TILE), full),
        *shapes[:3],
    )
    return call(
        attend_kernel, shapes, scratch, 8 * 10**9, *operands, anywhere=(0, 1, 2, 3), saved=3
    )


def attend_back(*operands):
    low, full = jnp.bfloat16, jnp.float32
    shapes = (
        ((PAIRS, ROWS, 128), low),
        ((PAIRS, ROWS, 128), low),
        ((2, WIDTH, SIDE_END), low),
        ((2 * TILE, HALF), low),
    )
    scratch = (
        ((4 * TILE, ROWS), full),
        ((9, CHUNK, CHUNK), full),
        ((48, TILE), full),
        ((2, TILE, WIDTH), low),
        ((2 * TILE, HALF), low),
        ((4 * TILE, 128), low),
        ((4 * TILE, 128), low),
        ((4 * TILE, 1), full),
        ((4 * TILE, 1), full),
        ((128, 4 * TILE), low),
        ((128, 4 * TILE), low),
        ((128, ROWS), full),
        ((128, ROWS), full),
        ((PAIRS, ROWS, 128), low),
        ((PAIRS, ROWS, 128), low),
        ((PAIRS, 2 * TILE, 2 * TILE), full),
        ((WIDTH, ROWS), low),
        ((WIDTH, 2 * TILE), low),
        *shapes[:3],
        shapes[3],
        ((2, TILE, HALF), low),
        ((4 * TILE, 128), full),
        ((WIDTH, 128), low),
        ((WIDTH, HALF), low),
        ((WIDTH, HALF), low),
    )
    return call(
        back_kernel, shapes, scratch, 12 * 10**9, *operands, anywhere=range(13), saved=3
    )


def mid(rows, *operands):
    low, full = jnp.bfloat16, jnp.float32
    shapes = (((TILE, WIDTH), full), ((TILE, WIDTH), low), ((rows, WIDTH), low))
    return call(mid_kernel, shapes, (), 10**9, *operands)


def token_side(*operands):
    low, full = jnp.bfloat16, jnp.float32
    shapes = (
        ((TILE, WIDTH), low),
        ((TILE, WIDTH), full),
        ((TILE, WIDTH), low),
        ((WIDTH, 128), low),
    )
    return call(token_kernel, shapes, (), 10**9, None, *operands)


def up_pass(rows, hidden_units, *operands):
    (up,) = call(up_kernel, (((rows, hidden_units), jnp.bfloat16),), (), 3 * 10**9, *operands)
    return up


def spread(*operands):
    low = jnp.bfloat16
    shapes = (((8, TILE, WIDTH), low),) * 2
    scratch = (
        ((PAIRS, ROWS, 128), low),
        ((PAIRS, ROWS, 128), low),
        ((2, WIDTH, SIDE_END), low),
        ((ROWS, WIDTH), low),
    )
    return call(
        spread_kernel, shapes, scratch, 3 * 10**9, *operands, anywhere=(1, 2, 3), saved=2
    )


def by_rows(kernel, outs, scratch, flops, place, blocked, whole):
    count, block = blocked[0].shape[0], EXPERT_BLOCK
    low = jnp.bfloat16

    def spec(columns):
        return pl.BlockSpec((block, columns), lambda i: (i, 0))

    return pl.pallas_call(
        kernel,
        grid=(count // block,),
        out_shape=tuple(jax.ShapeDtypeStruct((count, columns), low) for columns in outs),
        in_specs=[
            pl.BlockSpec(memory_space=pltpu.SMEM),
            *(spec(array.shape[1]) for array in blocked),
            *(pl.BlockSpec(memory_space=pltpu.VMEM) for _ in whole),
        ],
        out_specs=tuple(spec(columns) for columns in outs),
        scratch_shapes=[pltpu.VMEM((block, columns), low) for columns in scratch],
        compiler_params=pltpu.CompilerParams(vmem_limit_bytes=EXPERT_VMEM),
        cost_estimate=pl.CostEstimate(
            flops=flops, bytes_accessed=20 * 2**20, transcendentals=2 * 10**6
        ),
    )(place, *blocked, *whole)


def expert_pass(place, rows, partner, up, w_in, w_out, side):
    units = w_in.shape[1]
    (back,) = by_rows(
        expert_kernel,
        (2 * WIDTH,),
        (units, units),
        8 * 10**9,
        place,
        (rows, partner, up),
        (w_in, w_out, side),
    )
    return back


def expert_again(place, rows, partner, up, w_in, side):
    units = w_in.shape[1]
    return by_rows(
        again_kernel, (units, units), (), 3 * 10**9, place, (rows, partner, up), (w_in, side)
    )


def swap(shard):
    return lax.ppermute(shard, CORE, [(0, 1), (1, 0)])


def to_all(shard, axes):
    devices = lax.axis_size(axes)
    return lax.all_to_all(
        jnp.broadcast_to(shard[None], (devices, *shard.shape)), axes, 0, 0, tiled=True
    )


def quad_exchange(blocks):
    me = lax.axis_index(QUAD)
    got = [lax.dynamic_index_in_dim(blocks, me, 0, keepdims=False)]
    for step in range(1, 4):
        part = lax.dynamic_index_in_dim(blocks, me ^ step, 0, keepdims=False)
        got.append(lax.ppermute(part, QUAD, [(i, i ^ step) for i in range(4)]))
    rows = []
    for place in range(4):
        row = got[0]
        for step in range(1, 4):
            row = jnp.where(me ^ step == place, got[step], row)
        rows.append(row)
    return jnp.stack(rows)


def exchange(blocks, axes):
    return lax.all_to_all(blocks, axes, split_axis=0, concat_axis=0, tiled=True)


def gelu_parts(pre):
    root = math.sqrt(2.0 / math.pi)
    square = pre * pre
    curve = jnp.tanh(pre * (root + (root * 0.044715) * square))
    share = 0.5 + 0.5 * curve
    value = pre * share
    slope = share + value * (1.0 - share) * (2 * root + (6 * root * 0.044715) * square)
    return value, slope


def shards(
    tokens,
    cotangent,
    routes,
    w_query,
    w_key,
    w_value,
    w_output,
    w_router,
    gain_attn,
    gain_ffn,
    bias_table,
    w_in,
    w_out,
):
    f32, bf16 = jnp.float32, jnp.bfloat16
    core = lax.axis_index(CORE)
    chip = lax.axis_index(CHIPS)
    expert = lax.axis_index(SEQ_CTX)
    on_first = core == 0
    tok_count, model_width = tokens.shape[1:]
    local_rows = w_query.shape[0]
    expert_count = w_router.shape[1]
    place = jnp.stack([chip, core, expert]).astype(jnp.int32)

    own_tokens = tokens[0]
    mine = to_all(own_tokens, CHIPS)
    other = swap(mine)

    quarters = jnp.stack([jnp.stack([w_query, w_key]), jnp.stack([w_value, w_output])])
    quarters = quarters.reshape(2, 2, local_rows, 2, HALF).transpose(3, 0, 2, 1, 4)
    quarters = quarters.reshape(2, 2, local_rows, 2 * HALF)
    extra = jnp.concatenate(
        [
            w_router,
            gain_attn[:, None],
            gain_ffn[:, None],
            jnp.zeros((local_rows, 128 - expert_count - 2), bf16),
        ],
        axis=1,
    )
    own_routes = routes.reshape(-1, 128).astype(bf16)
    own_routes = jnp.pad(own_routes, ((0, local_rows - own_routes.shape[0]), (0, 0)))
    extra = jnp.stack([extra, own_routes])
    extra = jnp.broadcast_to(extra[None], (2, *extra.shape))
    packed_weights = jnp.concatenate([quarters, extra], axis=-1).reshape(4, local_rows, -1)
    group_rows = 4 * local_rows
    weight_rows = quad_exchange(packed_weights).reshape(group_rows, -1)
    all_weights = to_all(weight_rows, SAME_CORE).reshape(2, model_width, -1)
    own_table = lax.dynamic_slice_in_dim(bias_table, core * (HEADS // 2), HEADS // 2, 1)
    near = near_biases(own_table)

    route_ids = routes[0]
    capacity = max(2, 2 * TOP * tok_count // expert_count)
    flat_ids = route_ids.reshape(-1)
    flat_marks = (flat_ids[:, None] == jnp.arange(expert_count, dtype=jnp.int32)).astype(jnp.int32)
    earlier = jnp.cumsum(flat_marks, axis=0, dtype=jnp.int32) - flat_marks
    slot_ids = jnp.sum(earlier * flat_marks, axis=-1, dtype=jnp.int32)
    row_index = (flat_ids * capacity + slot_ids).reshape(tok_count, TOP)
    exp_count = lax.axis_size("exp")
    device_count = expert_count * exp_count
    slots = jnp.arange(device_count * capacity, dtype=jnp.int32)
    slots = slots // (exp_count * capacity) * capacity + slots % capacity
    pick = (row_index.T[:, :, None] == slots[None, None, :]).astype(bf16)
    pack = (row_index.T[:, None, :] == slots[None, :, None]).astype(bf16)

    def to_experts(rows):
        return exchange(rows.reshape(device_count, capacity, -1), SEQ_CTX_EXP)

    cot_own = cotangent[0]
    all_pack = pack[0] + pack[1]
    cot_rows = plain_dot(all_pack, cot_own).astype(bf16)
    near, cot_rows, other, all_weights = lax.optimization_barrier(
        (near, cot_rows, other, all_weights)
    )
    cot_there = to_experts(cot_rows)
    wo_half = all_weights[1, :, HALF:model_width]
    wo_other = swap(wo_half)

    normed_all, keys, values, queries, attended, log_totals, side = attend(
        place, mine, other, all_weights, near
    )

    attended_other = swap(attended)
    pair_attended = jnp.concatenate(
        [
            jnp.where(on_first, attended, attended_other),
            jnp.where(on_first, attended_other, attended),
        ],
        axis=-1,
    )
    hidden, normed_ffn, packed = mid(
        device_count * capacity,
        place,
        attended,
        attended_other,
        own_tokens,
        side,
        wo_half,
        wo_other,
        all_pack,
    )
    there = to_experts(packed)

    inner_in, inner_out = w_in[0], w_out[0]
    flat_rows = there.reshape(-1, model_width)
    flat_cot = cot_there.reshape(flat_rows.shape[0], -1)
    all_routes = all_weights[1, :, model_width:].reshape(device_count, local_rows, 128)
    all_routes = all_routes[:, : TOP * tok_count // 128].reshape(device_count, -1)
    all_routes = all_routes.astype(jnp.int32)
    here = all_routes == expert
    rank = jnp.cumsum(here.astype(jnp.int32), axis=1, dtype=jnp.int32) - 1
    partners = jnp.flip(all_routes.reshape(device_count, -1, TOP), axis=2)
    partners = partners.reshape(device_count, 1, -1)
    in_slot = here[:, None, :] & (
        rank[:, None, :] == jnp.arange(capacity, dtype=jnp.int32)[None, :, None]
    )
    partner = jnp.sum(jnp.where(in_slot, partners, 0), axis=2, dtype=jnp.int32)
    partner = jnp.broadcast_to(partner.reshape(-1, 1), (device_count * capacity, 128)).astype(bf16)

    flat_cot, partner = lax.optimization_barrier((flat_cot, partner))
    up = up_pass(flat_rows.shape[0], inner_in.shape[1], place, flat_cot, inner_out)
    sent_back = expert_pass(place, flat_rows, partner, up, inner_in, inner_out, side)
    returned = exchange(sent_back.reshape(device_count, capacity, -1), SEQ_CTX_EXP)
    gated, d_pre = expert_again(place, flat_rows, partner, up, inner_in, side)
    grad_out_local = rows_dot(gated, flat_cot)
    grad_in_local = rows_dot(flat_rows, d_pre)
    normed_t = normed_all.T
    att_t = pair_attended.reshape(2 * tok_count, model_width).T

    returned, grad_out_local, grad_in_local, normed_t, att_t = lax.optimization_barrier(
        (returned, grad_out_local, grad_in_local, normed_t, att_t)
    )
    output, d_hidden, d_mixed, sums_side = token_side(
        returned.reshape(device_count * capacity, -1),
        pick.reshape(TOP * tok_count, -1),
        hidden,
        normed_ffn,
        cot_own,
        route_ids,
        side,
    )
    d_mixed_other = swap(d_mixed)

    d_keys, d_values, to_sum, d_queries = attend_back(
        place,
        queries,
        keys,
        values,
        attended,
        d_mixed,
        d_mixed_other,
        log_totals,
        near,
        normed_t,
        att_t,
        sums_side,
        wo_half,
        wo_other,
    )
    groups = model_width // group_rows
    to_add = exchange(to_sum.reshape(2 * groups, group_rows, -1), SAME_CORE)
    kept, given = spread(place, d_queries, d_keys, d_values, all_weights)
    chip_sums = (kept.astype(f32) + swap(given).astype(f32)).astype(bf16)
    to_add, chip_sums = lax.optimization_barrier((to_add, chip_sums))
    d_normed = jnp.sum(exchange(chip_sums, CHIPS).astype(f32), axis=0)
    summed = jnp.sum(to_add.astype(f32), axis=0)
    source = own_tokens.astype(f32)
    inv_first = lax.rsqrt(jnp.mean(source * source, axis=-1, keepdims=True) + epsilon)
    scaled_first = side[:, expert_count].astype(f32)[None, :] * d_normed
    grad_tokens = (
        d_hidden
        + inv_first * scaled_first
        - source * inv_first**3 * jnp.mean(scaled_first * source, axis=-1, keepdims=True)
    )

    cells = jnp.broadcast_to(
        summed[None, :, model_width:].reshape(1, 1, -1), (4, 1, 128 * group_rows)
    )
    cells = jnp.pad(cells, ((0, 0), (0, 0), (0, -cells.shape[2] % summed.shape[1])))
    finals = quad_exchange(
        jnp.concatenate(
            [summed.reshape(4, local_rows, -1), cells.reshape(4, -1, summed.shape[1])], axis=1
        )
    )
    finals = finals.reshape(2, 2, -1, summed.shape[1])
    body = finals[:, :, :local_rows]

    def both(part, begin):
        return jnp.concatenate(
            [body[0, part, :, begin : begin + HALF], body[1, part, :, begin : begin + HALF]], axis=1
        )

    grad_query, grad_key, grad_value, grad_output = both(0, 0), both(0, HALF), both(1, 0), both(1, HALF)
    grad_gain_attn = (
        jnp.sum(
            grad_query * w_query.astype(f32)
            + grad_key * w_key.astype(f32)
            + grad_value * w_value.astype(f32),
            axis=1,
        )
        / gain_attn.astype(f32)
    )
    last = body[0, 0, :, model_width:] + body[1, 0, :, model_width:]
    profile = finals[:, 1, local_rows:].reshape(2, -1)[:, : 128 * group_rows]
    profile = profile.reshape(HEADS, 2, 2 * TILE).sum(axis=1)
    far = (TILE - np.arange(2 * TILE)) % (2 * TILE)
    bucket = sum((far >= border).astype(np.int32) for border in limits())
    marks = (bucket[:, None] == np.arange(BUCKETS)).astype(np.float32)
    grad_table = lax.dot_general(
        jnp.asarray(marks), profile, (((0,), (1,)), ((), ())), precision=precise
    )
    return (
        output[None],
        grad_tokens[None],
        grad_query,
        grad_key,
        grad_value,
        grad_output,
        last[:, :expert_count],
        grad_gain_attn,
        last[:, expert_count],
        grad_table,
        grad_in_local[None],
        grad_out_local[None],
    )


def solution(mesh):
    split = Mesh(
        mesh.devices.reshape(mesh.shape["seq"], 2, 4, 2, mesh.shape["exp"]),
        ("seq", "ctx_0", "ctx_1", "ctx_2", "exp"),
    )
    in_specs = (
        P(("seq", "exp"), CTX, None),
        P(("seq", "exp"), CTX, None),
        P(("seq", "exp"), CTX, None),
        P(SEQ_CTX_EXP, None),
        P(SEQ_CTX_EXP, None),
        P(SEQ_CTX_EXP, None),
        P(SEQ_CTX_EXP, None),
        P(SEQ_CTX_EXP, None),
        P(SEQ_CTX_EXP),
        P(SEQ_CTX_EXP),
        P(),
        P(SEQ_CTX, None, "exp"),
        P(SEQ_CTX, "exp", None),
    )
    out_specs = (
        P(("seq", "exp"), CTX, None),
        P(("seq", "exp"), CTX, None),
        P(SEQ_CTX_EXP, None),
        P(SEQ_CTX_EXP, None),
        P(SEQ_CTX_EXP, None),
        P(SEQ_CTX_EXP, None),
        P(SEQ_CTX_EXP, None),
        P(SEQ_CTX_EXP),
        P(SEQ_CTX_EXP),
        P(),
        P(SEQ_CTX, None, "exp"),
        P(SEQ_CTX, "exp", None),
    )
    return jax.shard_map(
        shards, mesh=split, in_specs=in_specs, out_specs=out_specs, check_vma=False
    )
```
